256 devices in a mesh: dp: 8 (over z_hi, y), px: 4 (over x), py: 8 (over z_lo, core).
Axes of the slice: x: 4, y: 4, z: 8 (z_hi: 2, z_lo: 4; z = z_hi * 4 + z_lo), core: 2. Of those that a mesh axis runs over, the one named last changes fastest.
Arguments:
- fields: bfloat16 [8, 24, 128, 128, 128], P('dp', None, 'px', 'py'), may hold values from -6 to 6
- cotangent: bfloat16 [8, 24, 128, 128, 128], P('dp', None, 'px', 'py'), may hold values from -6 to 6
- spectral_weight: bfloat16 [1024, 16, 2, 576], P(('px', 'py')), may hold values from -6 to 6
- bypass: bfloat16 [24, 24], replicated, may hold values from -1.25 to 1.25
Outputs:
- grad_weight: float32 [1024, 16, 2, 576], P(('px', 'py'))
- grad_fields: bfloat16 [8, 24, 128, 128, 128], P('dp', None, 'px', 'py')
The draws below stay inside these ranges and needn't reach their ends.
All inputs are finite; a program needn't handle non-finite values.
Results may differ from the reference program's by a relative error of at most 0.025.
Values may be sent and summed in bfloat16 or wider, within the bound.
A program may use at most 192 MiB of HBM per device.

```python
import math
import jax
import jax.numpy as jnp
import numpy as np
from jax import lax

CH = 24
MODES = 16
NX = 128
NY = 128
NZ = 128
SAMP_DEV = 1
SAMPLES = 8
N_DP = 8


def level_of(key, extent, pieces, least, top_value):
    def one(axis_at, shards_of):
        draws = jax.random.uniform(jax.random.fold_in(jax.random.fold_in(key, 6), axis_at), (shards_of,), jnp.float32, least / len(pieces), top_value / len(pieces))
        return jnp.repeat(jnp.exp(draws), extent[axis_at] // shards_of).reshape((-1,) + (1,) * (len(extent) - axis_at - 1))

    gain = one(*pieces[0])
    for cut in pieces[1:]:
        gain = gain * one(*cut)
    return gain


def scatter_about(stream_key, dims, spread, most, pieces=(), kind=jnp.bfloat16):
    array = jax.random.normal(stream_key, dims, jnp.float32) * spread
    if len(pieces) > 0:
        array = level_of(stream_key, dims, pieces, -0.22, 0.18) * array
    return jnp.clip(array, min=-most, max=most).astype(kind)


def setup_inputs(seed: int = 0) -> dict:
    streams_of = jax.random.split(jax.random.key(seed), 5)
    return {
        "fields": scatter_about(streams_of[0], (SAMPLES, CH, NX, NY, NZ), 1.0, 6.0, ((0, 8), (2, 4), (3, 8))),
        "cotangent": scatter_about(streams_of[1], (SAMPLES, CH, NX, NY, NZ), 1.0, 6.0, ((0, 8), (2, 4), (3, 8))),
        "spectral_weight": scatter_about(streams_of[2], (4 * MODES * MODES, MODES, 2, CH * CH), 1.0, 6.0, ((0, 32),)),
        "bypass": scatter_about(streams_of[3], (CH, CH), CH ** -0.5, 1.25),
    }


def axis_table(length, mode_count):
    grid_pos = np.arange(length)
    kept_freq = np.concatenate([np.arange(mode_count), np.arange(length - mode_count, length)])
    angles = 2.0 * math.pi * ((kept_freq[None, :] * grid_pos[:, None]) % length) / length
    norm_scale = length ** -0.5
    cosine = np.cos(angles) * norm_scale
    sine_part = np.sin(angles) * norm_scale
    result = np.zeros((2, length, 2, 2 * mode_count))
    result[0, :, 0, :] = cosine
    result[1, :, 0, :] = sine_part
    result[0, :, 1, :] = -sine_part
    result[1, :, 1, :] = cosine
    return jnp.asarray(result, jnp.float32).astype(jnp.bfloat16)


def depth_tables(length, mode_count):
    grid_pos = np.arange(length)
    frequency = np.arange(mode_count)
    angles = 2.0 * math.pi * ((frequency[None, :] * grid_pos[:, None]) % length) / length
    norm_scale = length ** -0.5
    result = np.zeros((length, mode_count, 2))
    result[:, :, 0] = np.cos(angles) * norm_scale
    result[:, :, 1] = -np.sin(angles) * norm_scale
    result = result.reshape(length, 2 * mode_count)
    doubling = np.repeat(np.where(frequency == 0, 1.0, 2.0), 2)
    plain = jnp.asarray(result, jnp.float32).astype(jnp.bfloat16)
    doubled = jnp.asarray(result * doubling[None, :], jnp.float32).astype(jnp.bfloat16)
    return plain, doubled


def gelu_slope(values):
    normal_cdf = 0.5 * (1.0 + lax.erf(values * 0.7071067811865476))
    density = jnp.exp(-0.5 * values * values) * 0.3989422804014327
    return normal_cdf + values * density


def product(form, left, right):
    return jnp.einsum(form, left.astype(jnp.float32), right.astype(jnp.float32), precision=lax.Precision.HIGHEST)


def to_modes(source, depth_cut, cross_cut, along_cut):
    channels = source.shape[0]
    lines = product('cxyn,nq->cqxy', source, depth_cut).astype(jnp.bfloat16)
    lines = lines.reshape(channels, MODES, 2, NX, NY)
    row_modes = product('czrxy,rysk->czsxk', lines, along_cut).astype(jnp.bfloat16)
    return product('czsxk,sxtj->cztjk', row_modes, cross_cut).astype(jnp.bfloat16)


def from_modes(spectrum, depth_cut, cross_cut, along_cut):
    channels = spectrum.shape[0]
    row_modes = product('cztjk,rxtj->czrxk', spectrum, cross_cut).astype(jnp.bfloat16)
    plane_vals = product('czsxk,rysk->czrxy', row_modes, along_cut).astype(jnp.bfloat16)
    plane_vals = plane_vals.reshape(channels, 2 * MODES, NX, NY)
    return product('cqxy,nq->cxyn', plane_vals, depth_cut)


def reference(fields, cotangent, spectral_weight, bypass):
    depth_cut, depth_double = depth_tables(NZ, MODES)
    cross_cut = axis_table(NX, MODES)
    along_cut = axis_table(NY, MODES)
    mode_total = 4 * MODES * MODES
    weights = spectral_weight.reshape(mode_total, MODES, 2, CH, CH)
    weight_re = weights[:, :, 0]
    weight_im = weights[:, :, 1]
    running = jnp.zeros((mode_total, MODES, 2, CH * CH), jnp.float32)
    outputs = []
    for shard_index in range(N_DP):
        partial_sum = jnp.zeros((mode_total, MODES, 2, CH * CH), jnp.float32)
        for sample_index in range(SAMP_DEV):
            index = shard_index * SAMP_DEV + sample_index
            source = fields[index]
            field_hat = to_modes(source, depth_cut, cross_cut, along_cut).reshape(CH, MODES, 2, mode_total)
            field_re = field_hat[:, :, 0]
            field_im = field_hat[:, :, 1]
            mixed_re = product('mzio,izm->ozm', weight_re, field_re) - product('mzio,izm->ozm', weight_im, field_im)
            mixed_im = product('mzio,izm->ozm', weight_re, field_im) + product('mzio,izm->ozm', weight_im, field_re)
            mixed_hat = jnp.stack([mixed_re, mixed_im], axis=2).astype(jnp.bfloat16)
            spatial = from_modes(mixed_hat.reshape(CH, MODES, 2, 2 * MODES, 2 * MODES), depth_double, cross_cut, along_cut)
            pre_act = spatial + product('oc,cxyn->oxyn', bypass, source)
            gprime = (cotangent[index].astype(jnp.float32) * gelu_slope(pre_act)).astype(jnp.bfloat16)
            grad_hat = to_modes(gprime, depth_double, cross_cut, along_cut).reshape(CH, MODES, 2, mode_total)
            grad_re = grad_hat[:, :, 0]
            grad_im = grad_hat[:, :, 1]
            part_real = product('ozm,izm->mzio', grad_re, field_re) + product('ozm,izm->mzio', grad_im, field_im)
            part_imag = product('ozm,izm->mzio', grad_im, field_re) - product('ozm,izm->mzio', grad_re, field_im)
            partial_sum = partial_sum + jnp.stack([part_real, part_imag], axis=2).reshape(mode_total, MODES, 2, CH * CH)
            back_re = product('mzio,ozm->izm', weight_re, grad_re) + product('mzio,ozm->izm', weight_im, grad_im)
            back_im = product('mzio,ozm->izm', weight_re, grad_im) - product('mzio,ozm->izm', weight_im, grad_re)
            back_hat = jnp.stack([back_re, back_im], axis=2).astype(jnp.bfloat16)
            returned = from_modes(back_hat.reshape(CH, MODES, 2, 2 * MODES, 2 * MODES), depth_cut, cross_cut, along_cut)
            returned = returned + product('oc,oxyn->cxyn', bypass, gprime)
            outputs.append(returned.astype(jnp.bfloat16))
        rounded = lax.optimization_barrier(partial_sum.astype(jnp.bfloat16))
        running = running + rounded.astype(jnp.float32)
    return running, jnp.stack(outputs)
```

```python
import functools
import math

import jax
import jax.numpy as jnp
import ml_dtypes
import numpy as np
from jax import lax
from jax.experimental import pallas as pl
from jax.experimental.pallas import tpu as pltpu
from jax.sharding import PartitionSpec as P

MODES = 16
NX = 128
NY = 128
NZ = 128
CH = 24
PX = 4
PY = 8
DP = 8
XL = NX // PX
YL = NY // PY
CELLS = XL * YL
GROUPS = 3
GC = CH // GROUPS
LANES = GC * MODES
KX = 2 * MODES
KY = 2 * MODES
ROWS = 2 * KY
BLOCK = PY * 2 * YL
PIECE = 2 * YL
IO = CH * CH
MESH = pl.DeviceIdType.MESH
F32 = jnp.float32
BF16 = jnp.bfloat16


def bf(array):
    return np.asarray(array, np.float32).astype(ml_dtypes.bfloat16)


def axis_table(length, mode_count):
    grid_pos = np.arange(length)
    kept_freq = np.concatenate([np.arange(mode_count), np.arange(length - mode_count, length)])
    angles = 2.0 * math.pi * (kept_freq[None, :] * grid_pos[:, None] % length) / length
    norm_scale = length ** (-0.5)
    cosine = np.cos(angles) * norm_scale
    sine_part = np.sin(angles) * norm_scale
    result = np.zeros((2, length, 2, 2 * mode_count))
    result[0, :, 0, :] = cosine
    result[1, :, 0, :] = sine_part
    result[0, :, 1, :] = -sine_part
    result[1, :, 1, :] = cosine
    return result


def depth_tables(length, mode_count):
    grid_pos = np.arange(length)
    frequency = np.arange(mode_count)
    angles = 2.0 * math.pi * (frequency[None, :] * grid_pos[:, None] % length) / length
    norm_scale = length ** (-0.5)
    result = np.zeros((length, mode_count, 2))
    result[:, :, 0] = np.cos(angles) * norm_scale
    result[:, :, 1] = -np.sin(angles) * norm_scale
    doubling = np.where(frequency == 0, 1.0, 2.0)
    return result, result * doubling[None, :, None]


@functools.cache
def tables():
    plain, doubled = depth_tables(NZ, MODES)

    def depth(table):
        out = np.zeros((GC, NZ, 2, GC, MODES))
        for c in range(GC):
            out[c, :, :, c, :] = table.transpose(0, 2, 1)
        return out.reshape(GC * NZ, 2 * LANES)

    dz, dh = depth(plain), depth(doubled)
    cross = axis_table(NX, MODES).reshape(2, PX, XL, 2, KX)
    m1 = np.zeros((PX, KX, 2, YL, 2, XL, YL))
    for y in range(YL):
        m1[:, :, :, y, :, :, y] = cross.transpose(1, 4, 3, 0, 2)
    m1 = m1.reshape(PX, KX * 2 * YL, 2 * CELLS)
    along = axis_table(NY, MODES).reshape(2, PY, YL, 2, KY)
    my = along.transpose(3, 4, 1, 0, 2).reshape(ROWS, BLOCK)
    sel = np.zeros((CH, MODES, MODES, 128))
    for c in range(CH):
        for k in range(MODES):
            sel[c, k, k, c] = 1.0
    sel = sel.reshape(CH * MODES, MODES * 128)
    exp_i = np.zeros((128, CH, CH))
    exp_o = np.zeros((128, CH, CH))
    for c in range(CH):
        exp_i[c, c, :] = 1.0
        exp_o[c, :, c] = 1.0
    exp_i = exp_i.reshape(128, IO)
    exp_o = exp_o.reshape(128, IO)
    rep = np.zeros((CH * YL, CH))
    for c in range(CH):
        rep[c * YL : (c + 1) * YL, c] = 1.0
    return dict(
        dz=bf(dz), dh=bf(dh), dzt=bf(dz.T), dht=bf(dh.T),
        m1=bf(m1), m1t=bf(m1.transpose(0, 2, 1)),
        my=bf(my), myt=bf(my.T), sel=bf(sel), place=bf(sel.T),
        exp_i=bf(exp_i), exp_o=bf(exp_o), sum_i=bf(exp_i.T), sum_o=bf(exp_o.T),
        rep=bf(rep), rept=bf(rep.T),
    )


NAMES = (
    "dz", "m1", "rep", "rept", "my", "sel", "exp_i", "sum_o", "place", "myt", "m1t", "dht", "dh",
    "exp_o", "sum_i", "dzt",
)


def dot(a, b):
    return jnp.dot(a, b, preferred_element_type=F32)


def gelu_slope(values):
    normal_cdf = 0.5 * (1.0 + lax.erf(values * 0.7071067811865476))
    density = jnp.exp(-0.5 * values * values) * 0.3989422804014327
    return normal_cdf + values * density


def kernel(*refs):
    fields_h, cot_h, w_h, byp = refs[:4]
    tab_h = dict(zip(NAMES, refs[4 : 4 + len(NAMES)]))
    refs = refs[4 + len(NAMES) :]
    gw_h, gf_h = refs[:2]
    refs = refs[2:]
    tab = dict(zip(NAMES, refs[: len(NAMES)]))
    (
        fields, cot, gp, w, pb, out, bypk, bypkt, xbuf, tbuf, ybuf, rs, sbuf, rbuf, vbuf, ag, dpu, dpg,
        ue, ge, prod, us, gs, gw,
        load_sem, store_sem, rs_s, rs_r, a2_s, a2_r, ag_s, ag_r, dp_s, dp_r,
    ) = refs[len(NAMES) :]

    px = lax.axis_index("px")
    py = lax.axis_index("py")
    dp = lax.axis_index("dp")
    zhi = dp // 4
    yy = lax.rem(dp, 4)

    loads = {}

    def load(name, src, dst, index):
        copy = pltpu.make_async_copy(src, dst, load_sem.at[index])
        copy.start()
        loads[name] = copy

    load("f0", fields_h.at[pl.ds(0, GC)], fields.at[pl.ds(0, GC)], 0)
    load("dz", tab_h["dz"], tab["dz"], 1)
    load("m1", tab_h["m1"].at[px], tab["m1"], 2)
    load("f1", fields_h.at[pl.ds(GC, GC)], fields.at[pl.ds(GC, GC)], 3)
    load("f2", fields_h.at[pl.ds(2 * GC, GC)], fields.at[pl.ds(2 * GC, GC)], 4)
    load("w", w_h, w, 5)
    index = 6
    for name in NAMES[2:]:
        src = tab_h[name].at[px] if name == "m1t" else tab_h[name]
        load(name, src, tab[name], index)
        index += 1
    load("cot", cot_h, cot, index)
    waited = set()

    def need(*names):
        for name in names:
            if name not in waited:
                loads[name].wait()
                waited.add(name)

    def at_px(j):
        return {"px": lax.rem(px + j, PX)}

    def at_py(k):
        return {"py": lax.rem(py + k, PY)}

    def at_y(j):
        return {"dp": zhi * 4 + lax.rem(yy + j, 4)}

    far = {"dp": lax.rem(dp + 4, DP)}
    partners = [at_px(j) for j in range(1, PX)] + [at_py(k) for k in range(1, PY)]
    partners += [at_y(j) for j in range(1, 4)] + [far]
    barrier = pltpu.get_barrier_semaphore()
    for where in partners:
        pl.semaphore_signal(barrier, inc=1, device_id=where, device_id_type=MESH)

    sends = []

    def send(src, dst, send_sem, recv_sem, where):
        copy = pltpu.make_async_remote_copy(
            src_ref=src, dst_ref=dst, send_sem=send_sem, recv_sem=recv_sem,
            device_id=where, device_id_type=MESH,
        )
        copy.start()
        sends.append(copy)
        return copy

    rs_c, a2_c, ag_c, dp_c = {}, {}, {}, {}

    def cross_and_send(t, g):
        for j in (2, 1, 3, 0):
            dest = lax.rem(px + j, PX)
            rows = pl.ds(pl.multiple_of(dest * BLOCK, BLOCK), BLOCK)
            ybuf[t, g, rows, :] = dot(tab["m1"][rows, :], xbuf[...]).astype(BF16)
            if j:
                rs_c[t, g, j] = send(
                    ybuf.at[t, g, rows], rs.at[t, g, j - 1], rs_s.at[t, g, j - 1], rs_r.at[t, g, j - 1], at_px(j)
                )

    def depth_rows(r, lhs, table):
        part = dot(lhs, table).astype(BF16)
        n = lhs.shape[0]
        xbuf[pl.ds(pl.multiple_of(r * n, n), n), :] = part[:, :LANES]
        xbuf[pl.ds(pl.multiple_of(CELLS + r * n, n), n), :] = part[:, LANES:]

    def reduce_and_send(t, g):
        for j in range(1, PX):
            rs_c[t, g, j].wait_recv()
        own = pl.ds(pl.multiple_of(px * BLOCK, BLOCK), BLOCK)
        total = ybuf[t, g, own, :].astype(F32)
        for j in range(1, PX):
            total = total + rs[t, g, j - 1].astype(F32)
        sbuf[t, g] = total.astype(BF16)
        mine = pl.ds(pl.multiple_of(py * PIECE, PIECE), PIECE)
        for k in range(1, PY):
            dest = lax.rem(py + k, PY)
            rows = pl.ds(pl.multiple_of(dest * PIECE, PIECE), PIECE)
            a2_c[2 * t, g, k] = send(
                sbuf.at[t, g, rows], rbuf.at[t, g, mine], a2_s.at[2 * t, g, k - 1], a2_r.at[2 * t, g, k - 1], at_py(k)
            )
        rbuf[t, g, mine, :] = sbuf[t, g, mine, :]

    def spectrum(t):
        for g in range(GROUPS):
            for k in range(1, PY):
                a2_c[2 * t, g, k].wait_recv()
        lines = jnp.concatenate([rbuf[t, g] for g in range(GROUPS)], axis=1)
        return dot(tab["my"][...], lines).astype(BF16)

    def spread(hat, sel_to, expand, target):
        chosen = dot(hat, tab["sel"][...]).astype(BF16)
        for k in range(MODES):
            sel_to[pl.ds(k * ROWS, ROWS), :] = chosen[:, k * 128 : (k + 1) * 128]

        def body(b, _):
            rows = pl.ds(pl.multiple_of(b * 256, 256), 256)
            target[rows, :] = dot(sel_to[rows, :], expand[...]).astype(BF16)
            return 0

        lax.fori_loop(0, 4, body, 0)

    def mix(target, conj, collapse):
        def body(k, _):
            re = pl.ds(pl.multiple_of(k * ROWS, ROWS), KY)
            im = pl.ds(pl.multiple_of(k * ROWS + KY, KY), KY)
            w_re, w_im = w[re, :].astype(F32), w[im, :].astype(F32)
            u_re, u_im = target[re, :].astype(F32), target[im, :].astype(F32)
            if conj:
                prod[re, :] = (w_re * u_re + w_im * u_im).astype(BF16)
                prod[im, :] = (w_re * u_im - w_im * u_re).astype(BF16)
            else:
                prod[re, :] = (w_re * u_re - w_im * u_im).astype(BF16)
                prod[im, :] = (w_re * u_im + w_im * u_re).astype(BF16)
            return 0

        lax.fori_loop(0, MODES, body, 0)
        summed = dot(prod[...], collapse[...]).astype(BF16)
        wide = jnp.concatenate([summed[k * ROWS : (k + 1) * ROWS] for k in range(MODES)], axis=1)
        return dot(wide, tab["place"][...]).astype(BF16)

    own_block = pl.ds(pl.multiple_of(px * BLOCK, BLOCK), BLOCK)

    def inverse_send(t, mixed):
        lines = dot(tab["myt"][...], mixed).astype(BF16)
        mine = pl.ds(pl.multiple_of(px * BLOCK + py * PIECE, PIECE), PIECE)
        for g in range(GROUPS):
            vbuf[t, g] = lines[:, g * LANES : (g + 1) * LANES]
            for k in range(1, PY):
                dest = lax.rem(py + k, PY)
                rows = pl.ds(pl.multiple_of(dest * PIECE, PIECE), PIECE)
                a2_c[2 * t + 1, g, k] = send(
                    vbuf.at[t, g, rows], ag.at[t, g, mine],
                    a2_s.at[2 * t + 1, g, k - 1], a2_r.at[2 * t + 1, g, k - 1], at_py(k),
                )
            here = pl.ds(pl.multiple_of(py * PIECE, PIECE), PIECE)
            ag[t, g, mine, :] = vbuf[t, g, here, :]

    def gather_send(t, g):
        for k in range(1, PY):
            a2_c[2 * t + 1, g, k].wait_recv()
        for j in (2, 1, 3):
            ag_c[t, g, j] = send(
                ag.at[t, g, own_block], ag.at[t, g, own_block], ag_s.at[t, g, j - 1], ag_r.at[t, g, j - 1], at_px(j)
            )

    def cross_back(t, g):
        for j in range(1, PX):
            ag_c[t, g, j].wait_recv()

        def body(b, _):
            rows = pl.ds(pl.multiple_of(b * 256, 256), 256)
            tbuf[rows, :] = dot(tab["m1t"][rows, :], ag[t, g]).astype(BF16)
            return 0

        lax.fori_loop(0, 4, body, 0)

    CHUNK = 128

    def field_values(r, table):
        rows = pl.ds(pl.multiple_of(r * CHUNK, CHUNK), CHUNK)
        rows_im = pl.ds(pl.multiple_of(CELLS + r * CHUNK, CHUNK), CHUNK)
        return dot(jnp.concatenate([tbuf[rows, :], tbuf[rows_im, :]], axis=1), table)

    def bypass_all(matrix, source):
        def body(b, _):
            parts = []
            for e in range(2):
                rows = pl.ds(pl.multiple_of(b * 32 + e * 16, 16), 16)
                parts.append(source[:, rows, :].reshape(CH * YL, NZ))
            value = dot(matrix[...], jnp.concatenate(parts, axis=1))
            for e in range(2):
                rows = pl.ds(pl.multiple_of(b * 32 + e * 16, 16), 16)
                pb[:, rows, :] = value[:, e * NZ : (e + 1) * NZ].reshape(CH, YL, NZ)
            return 0

        lax.fori_loop(0, CELLS // 32, body, 0)

    need("f0", "dz", "m1")
    for g in range(GROUPS):
        need("f%d" % g)

        def body(r, _):
            rows = pl.ds(pl.multiple_of(r * 256, 256), 256)
            lhs = jnp.concatenate([fields[g * GC + c, rows, :] for c in range(GC)], axis=1)
            depth_rows(r, lhs, tab["dz"][...])
            return 0

        lax.fori_loop(0, 2, body, 0)
        if g == 0:
            pl.semaphore_wait(barrier, len(partners))
        cross_and_send(0, g)

    need("rep", "rept")
    mask = lax.rem(lax.broadcasted_iota(jnp.int32, (CH * YL, CH * YL), 0), YL) == lax.rem(
        lax.broadcasted_iota(jnp.int32, (CH * YL, CH * YL), 1), YL
    )
    left = dot(tab["rep"][...], byp[...]).astype(BF16)
    full = dot(left, tab["rept"][...])
    bypk[...] = jnp.where(mask, full, 0.0).astype(BF16)
    bypkt[...] = jnp.where(mask, full, 0.0).T.astype(BF16)

    reduce_and_send(0, 0)
    reduce_and_send(0, 1)
    bypass_all(bypk, fields)
    reduce_and_send(0, 2)

    need("my", "sel", "exp_i", "sum_o", "place", "myt", "w")
    u_hat = spectrum(0)
    dpu[0] = u_hat
    dp_c["u", 0] = send(dpu.at[0], dpu.at[1], dp_s.at[0, 0], dp_r.at[0, 0], far)
    spread(u_hat, us, tab["exp_i"], ue)
    inverse_send(0, mix(ue, False, tab["sum_o"]))
    need("m1t", "dht", "dh", "cot")
    for g in range(GROUPS):
        gather_send(0, g)
    dp_c["u", 0].wait_recv()
    for j in range(1, 4):
        dp_c["u", j] = send(dpu.at[pl.ds(0, 2)], dpu.at[pl.ds(2 * j, 2)], dp_s.at[0, j], dp_r.at[0, j], at_y(j))

    for g in range(GROUPS):
        cross_back(0, g)

        def body(r, _):
            values = field_values(r, tab["dht"][...])
            rows = pl.ds(pl.multiple_of(r * CHUNK, CHUNK), CHUNK)
            parts = []
            for c in range(GC):
                pre = values[:, c * NZ : (c + 1) * NZ] + pb[g * GC + c, rows, :]
                slope = gelu_slope(pre)
                part = (cot[g * GC + c, rows, :].astype(F32) * slope).astype(BF16)
                gp[g * GC + c, rows, :] = part
                parts.append(part)
            depth_rows(r, jnp.concatenate(parts, axis=1), tab["dh"][...])
            return 0

        lax.fori_loop(0, CELLS // CHUNK, body, 0)
        cross_and_send(1, g)
        if g:
            reduce_and_send(1, g - 1)
    bypass_all(bypkt, gp)
    reduce_and_send(1, GROUPS - 1)

    need("exp_o", "sum_i", "dzt")
    g_hat = spectrum(1)
    dpg[0] = g_hat
    dp_c["g", 0] = send(dpg.at[0], dpg.at[1], dp_s.at[1, 0], dp_r.at[1, 0], far)
    spread(g_hat, us, tab["exp_o"], ge)
    inverse_send(1, mix(ge, True, tab["sum_i"]))
    for g in range(GROUPS):
        gather_send(1, g)
    dp_c["g", 0].wait_recv()
    for j in range(1, 4):
        dp_c["g", j] = send(dpg.at[pl.ds(0, 2)], dpg.at[pl.ds(2 * j, 2)], dp_s.at[1, j], dp_r.at[1, j], at_y(j))

    def choose(source, target):
        rows_all = source[...].reshape(DP * ROWS, CH * MODES)
        for b in range(MODES // 2):
            cols = slice(b * 256, (b + 1) * 256)
            chosen = dot(rows_all, tab["sel"][:, cols]).astype(BF16)
            target[2 * b] = chosen[:, :128]
            target[2 * b + 1] = chosen[:, 128:]

    for j in range(1, 4):
        dp_c["u", j].wait_recv()
    choose(dpu, gs.at[0])
    for j in range(1, 4):
        dp_c["g", j].wait_recv()
    choose(dpg, gs.at[1])

    def gw_body(k, _):
        u_all = dot(gs[0, k], tab["exp_i"][...])
        g_all = dot(gs[1, k], tab["exp_o"][...])
        real = jnp.zeros((KY, IO), F32)
        imag = jnp.zeros((KY, IO), F32)
        for d in range(DP):
            u_re, u_im = u_all[d * ROWS : d * ROWS + KY], u_all[d * ROWS + KY : (d + 1) * ROWS]
            g_re, g_im = g_all[d * ROWS : d * ROWS + KY], g_all[d * ROWS + KY : (d + 1) * ROWS]
            real += g_re * u_re + g_im * u_im
            imag += g_im * u_re - g_re * u_im
        gw[pl.ds(pl.multiple_of(k * ROWS, ROWS), KY), :] = real
        gw[pl.ds(pl.multiple_of(k * ROWS + KY, KY), KY), :] = imag
        return 0

    lax.fori_loop(0, MODES, gw_body, 0)
    stores = [pltpu.make_async_copy(gw, gw_h, store_sem.at[GROUPS])]
    stores[0].start()

    for g in range(GROUPS):
        cross_back(1, g)

        def body(r, _):
            values = field_values(r, tab["dzt"][...])
            rows = pl.ds(pl.multiple_of(r * CHUNK, CHUNK), CHUNK)
            for c in range(GC):
                total = values[:, c * NZ : (c + 1) * NZ] + pb[g * GC + c, rows, :]
                out[g * GC + c, rows, :] = total.astype(BF16)
            return 0

        lax.fori_loop(0, CELLS // CHUNK, body, 0)
        part = pl.ds(g * GC, GC)
        copy = pltpu.make_async_copy(out.at[part], gf_h.at[part], store_sem.at[g])
        copy.start()
        stores.append(copy)

    for copy in stores:
        copy.wait()
    for copy in sends:
        copy.wait_send()


def shards(fields, cotangent, spectral_weight, bypass):
    tab = tables()
    arrays = [jnp.asarray(tab[name]) for name in NAMES]
    w = spectral_weight.transpose(1, 2, 0, 3).reshape(MODES * ROWS, IO)
    any_spec = pl.BlockSpec(memory_space=pl.ANY)
    vmem = pltpu.VMEM
    shapes = [a.shape[1:] if name in ("m1", "m1t") else a.shape for name, a in zip(NAMES, arrays)]
    scratch = [vmem(shape, BF16) for shape in shapes] + [
        vmem((CH, CELLS, NZ), BF16),
        vmem((CH, CELLS, NZ), BF16),
        vmem((CH, CELLS, NZ), BF16),
        vmem((MODES * ROWS, IO), BF16),
        vmem((CH, CELLS, NZ), F32),
        vmem((CH, CELLS, NZ), BF16),
        vmem((CH * YL, CH * YL), BF16),
        vmem((CH * YL, CH * YL), BF16),
        vmem((2 * CELLS, LANES), BF16),
        vmem((2 * CELLS, LANES), BF16),
        vmem((2, GROUPS, PX * BLOCK, LANES), BF16),
        vmem((2, GROUPS, PX - 1, BLOCK, LANES), BF16),
        vmem((2, GROUPS, BLOCK, LANES), BF16),
        vmem((2, GROUPS, BLOCK, LANES), BF16),
        vmem((2, GROUPS, BLOCK, LANES), BF16),
        vmem((2, GROUPS, PX * BLOCK, LANES), BF16),
        vmem((DP, ROWS, CH * MODES), BF16),
        vmem((DP, ROWS, CH * MODES), BF16),
        vmem((MODES * ROWS, IO), BF16),
        vmem((MODES * ROWS, IO), BF16),
        vmem((MODES * ROWS, IO), BF16),
        vmem((MODES * ROWS, 128), BF16),
        vmem((2, MODES, DP * ROWS, 128), BF16),
        vmem((MODES * ROWS, IO), F32),
        pltpu.SemaphoreType.DMA((len(NAMES) + 5,)),
        pltpu.SemaphoreType.DMA((GROUPS + 1,)),
        pltpu.SemaphoreType.DMA((2, GROUPS, PX - 1)),
        pltpu.SemaphoreType.DMA((2, GROUPS, PX - 1)),
        pltpu.SemaphoreType.DMA((4, GROUPS, PY - 1)),
        pltpu.SemaphoreType.DMA((4, GROUPS, PY - 1)),
        pltpu.SemaphoreType.DMA((2, GROUPS, PX - 1)),
        pltpu.SemaphoreType.DMA((2, GROUPS, PX - 1)),
        pltpu.SemaphoreType.DMA((2, 4)),
        pltpu.SemaphoreType.DMA((2, 4)),
    ]
    gw, gf = pl.pallas_call(
        kernel,
        out_shape=(
            jax.ShapeDtypeStruct((MODES * ROWS, IO), F32),
            jax.ShapeDtypeStruct((CH, CELLS, NZ), BF16),
        ),
        in_specs=[any_spec] * 3 + [pl.BlockSpec(memory_space=pltpu.VMEM)] + [any_spec] * len(arrays),
        out_specs=(any_spec, any_spec),
        scratch_shapes=scratch,
        compiler_params=pltpu.CompilerParams(
            collective_id=0, has_side_effects=True, vmem_limit_bytes=60 * 1024 * 1024
        ),
        cost_estimate=pl.CostEstimate(flops=20_000_000_000, bytes_accessed=30_000_000, transcendentals=3_000_000),
    )(
        fields.reshape(CH, CELLS, NZ), cotangent.reshape(CH, CELLS, NZ), w, bypass, *arrays
    )
    grad_weight = gw.reshape(MODES, 2, KY, IO).transpose(2, 0, 1, 3)
    return grad_weight, gf.reshape(1, CH, XL, YL, NZ)


def solution(mesh):
    in_specs = (
        P("dp", None, "px", "py", None),
        P("dp", None, "px", "py", None),
        P(("px", "py"), None, None, None),
        P(),
    )
    out_specs = (P(("px", "py"), None, None, None), P("dp", None, "px", "py", None))
    return jax.shard_map(shards, mesh=mesh, in_specs=in_specs, out_specs=out_specs, check_vma=False)
```

```python
import functools
import math

import jax
import jax.numpy as jnp
import ml_dtypes
import numpy as np
from jax import lax
from jax.experimental import pallas as pl
from jax.experimental.pallas import tpu as pltpu
from jax.sharding import PartitionSpec as P

MODES = 16
NX = 128
NY = 128
NZ = 128
CH = 24
PX = 4
PY = 8
DP = 8
XL = NX // PX
YL = NY // PY
CELLS = XL * YL
GROUPS = 3
GC = CH // GROUPS
LANES = GC * MODES
KX = 2 * MODES
KY = 2 * MODES
ROWS = 2 * KY
BLOCK = PY * 2 * YL
PIECE = 2 * YL
IO = CH * CH
WIDE = 640
PATTERN = 384
ORDER = (2, 1, 3, 0)
HALF = MODES // 2
XROWS = 2 * PY
YLANES = YL * LANES
NEAR = DP // 2
CHUNK = 128
MESH = pl.DeviceIdType.MESH
F32 = jnp.float32
BF16 = jnp.bfloat16


def bf(array):
    return np.asarray(array, np.float32).astype(ml_dtypes.bfloat16)


def axis_table(length, mode_count):
    grid_pos = np.arange(length)
    kept_freq = np.concatenate([np.arange(mode_count), np.arange(length - mode_count, length)])
    angles = 2.0 * math.pi * (kept_freq[None, :] * grid_pos[:, None] % length) / length
    norm_scale = length ** (-0.5)
    cosine = np.cos(angles) * norm_scale
    sine_part = np.sin(angles) * norm_scale
    result = np.zeros((2, length, 2, 2 * mode_count))
    result[0, :, 0, :] = cosine
    result[1, :, 0, :] = sine_part
    result[0, :, 1, :] = -sine_part
    result[1, :, 1, :] = cosine
    return result


def depth_tables(length, mode_count):
    grid_pos = np.arange(length)
    frequency = np.arange(mode_count)
    angles = 2.0 * math.pi * (frequency[None, :] * grid_pos[:, None] % length) / length
    norm_scale = length ** (-0.5)
    result = np.zeros((length, mode_count, 2))
    result[:, :, 0] = np.cos(angles) * norm_scale
    result[:, :, 1] = -np.sin(angles) * norm_scale
    doubling = np.where(frequency == 0, 1.0, 2.0)
    return result, result * doubling[None, :, None]


@functools.cache
def tables():
    plain, doubled = depth_tables(NZ, MODES)

    def depth(table):
        out = np.zeros((GC, NZ, 2, GC, MODES))
        for c in range(GC):
            out[c, :, :, c, :] = table.transpose(0, 2, 1)
        return out.reshape(GC * NZ, 2 * LANES)

    dz, dh = depth(plain), depth(doubled)
    cross = axis_table(NX, MODES).reshape(2, PX, XL, 2, KX)
    m1 = cross.transpose(1, 4, 3, 0, 2).reshape(PX, KX * 2, 2 * XL)
    along = axis_table(NY, MODES).reshape(2, PY, YL, 2, KY)
    my = along.transpose(3, 4, 1, 0, 2).reshape(ROWS, BLOCK)
    sel = np.zeros((2, CH, MODES, MODES, 2, 32))
    for c in range(CH):
        for k in range(MODES):
            sel[0, c, k, k, 0, c] = 1.0
            sel[1, c, k, k, 1, c] = 1.0
    sel = sel.reshape(2 * CH * MODES, MODES * 64)
    exp_i = np.zeros((CH, CH, CH))
    exp_o = np.zeros((CH, CH, CH))
    for c in range(CH):
        exp_i[c, c, :] = 1.0
        exp_o[c, :, c] = 1.0
    exp_i = exp_i.reshape(CH, IO)
    exp_o = exp_o.reshape(CH, IO)
    expand = np.zeros((2, 2, 64, WIDE + PATTERN))
    sum_i = np.zeros((2, IO, 2, 64))
    sum_o = np.zeros((2, IO, 2, 64))
    for q in range(2):
        expand[q, q, :CH, :IO] = exp_i
        expand[q, q, 32 : 32 + CH, WIDE:] = exp_o[:, :PATTERN]
        sum_i[q, :, q, :CH] = exp_i.T
        sum_o[q, :, q, :CH] = exp_o.T
    expand = expand.reshape(2, 128, WIDE + PATTERN)
    sum_i = sum_i.reshape(2, IO, 128)
    sum_o = sum_o.reshape(2, IO, 128)
    turned = np.stack([
        m1[p].reshape(PX, XROWS, 2 * XL)[[(p + j) % PX for j in ORDER]].reshape(PX * XROWS, 2 * XL)
        for p in range(PX)
    ])
    rep = np.zeros((CH * YL, CH))
    for c in range(CH):
        rep[c * YL : (c + 1) * YL, c] = 1.0
    return dict(
        dz=bf(dz), dh=bf(dh), dzt=bf(dz.T), dht=bf(dh.T),
        m1=bf(turned), m1t=bf(m1.transpose(0, 2, 1)),
        my=bf(my), myt=bf(my.T), sel=bf(sel), place=bf(sel[: CH * MODES].T),
        expand=bf(expand), sum_i=bf(sum_i), sum_o=bf(sum_o),
        rep=bf(rep), rept=bf(rep.T),
    )


NAMES = (
    "dz", "m1", "m1t", "rep", "rept", "my", "sel", "expand", "sum_o", "place", "myt", "dht", "dh",
    "sum_i", "dzt",
)


def dot(a, b):
    return jnp.dot(a, b, preferred_element_type=F32)


def gelu_slope(values):
    normal_cdf = 0.5 * (1.0 + lax.erf(values * 0.7071067811865476))
    density = jnp.exp(-0.5 * values * values) * 0.3989422804014327
    return normal_cdf + values * density


def kernel(*refs):
    fields_h, cot_h, w_h, byp = refs[:4]
    tab_h = dict(zip(NAMES, refs[4 : 4 + len(NAMES)]))
    refs = refs[4 + len(NAMES) :]
    gw_h, gf_h = refs[:2]
    refs = refs[2:]
    tab = dict(zip(NAMES, refs[: len(NAMES)]))
    (
        fields, cot, gp, w4, w, pb, out, bypk, bypkt, xbuf, tbuf, zval, lines, turn, back, wide_ag, ybuf, rs, sbuf, rbuf, vbuf, ag, dpu, dpg,
        ue, prod, us, gs, wide, acc, gw,
        load_sem, store_sem, rs_s, rs_r, a2_s, a2_r, ag_s, ag_r, dp_s, dp_r,
    ) = refs[len(NAMES) :]

    px = lax.axis_index("px")
    py = lax.axis_index("py")
    dp = lax.axis_index("dp")
    zhi = dp // 4
    yy = lax.rem(dp, 4)

    loads = {}

    def load(name, src, dst, index):
        copy = pltpu.make_async_copy(src, dst, load_sem.at[index])
        copy.start()
        loads[name] = copy

    def load_later():
        for index, name in enumerate(NAMES[3:]):
            load(name, tab_h[name], tab[name], 7 + index)
        load("cot", cot_h, cot, 7 + len(NAMES) - 3)

    load("f0", fields_h.at[pl.ds(0, GC)], fields.at[pl.ds(0, GC)], 0)
    load("dz", tab_h["dz"], tab["dz"], 1)
    load("m1", tab_h["m1"].at[px], tab["m1"], 2)
    waited = set()

    def need(*names):
        for name in names:
            if name not in waited:
                loads[name].wait()
                waited.add(name)

    def at_px(j):
        return {"px": lax.rem(px + j, PX)}

    def at_py(k):
        return {"py": lax.rem(py + k, PY)}

    def at_y(j):
        return {"dp": zhi * 4 + lax.rem(yy + j, 4)}

    far = {"dp": lax.rem(dp + 4, DP)}
    partners = [at_px(j) for j in range(1, PX)] + [at_py(k) for k in range(1, PY)]
    partners += [at_y(j) for j in range(1, 4)] + [far]
    barrier = pltpu.get_barrier_semaphore()
    for where in partners:
        pl.semaphore_signal(barrier, inc=1, device_id=where, device_id_type=MESH)

    sends = []

    def send(src, dst, send_sem, recv_sem, where):
        copy = pltpu.make_async_remote_copy(
            src_ref=src, dst_ref=dst, send_sem=send_sem, recv_sem=recv_sem,
            device_id=where, device_id_type=MESH,
        )
        copy.start()
        sends.append(copy)
        return copy

    rs_c, a2_c, ag_c, dp_c = {}, {}, {}, {}

    def cross_and_send(t, g):
        made = dot(tab["m1"][...], xbuf[...]).astype(BF16)
        for pos, j in enumerate(ORDER):
            ybuf[t, g, pos] = made[pos * XROWS : (pos + 1) * XROWS]
            if j:
                rs_c[t, g, j] = send(
                    ybuf.at[t, g, pos], rs.at[t, g, j - 1], rs_s.at[t, g, j - 1], rs_r.at[t, g, j - 1], at_px(j)
                )

    def depth(source, g, table):
        lhs = jnp.concatenate([source[g * GC + c] for c in range(GC)], axis=1)
        part = dot(lhs, table[...])
        for s in range(2):
            lines[s] = part[:, s * LANES : (s + 1) * LANES]
        for y in range(YL):
            for s in range(2):
                xbuf[s * XL : (s + 1) * XL, y * LANES : (y + 1) * LANES] = lines[
                    s, pl.ds(y, XL, stride=YL), :
                ].astype(BF16)

    def reduce_and_send(t, g):
        for j in range(1, PX):
            rs_c[t, g, j].wait_recv()
        total = ybuf[t, g, ORDER.index(0)].astype(F32)
        for j in range(1, PX):
            total = total + rs[t, g, j - 1].astype(F32)
        for y in range(YL):
            turn[y * XROWS : (y + 1) * XROWS, :] = total[:, y * LANES : (y + 1) * LANES]
        for r in range(XROWS):
            sbuf[t, g, r * YL : (r + 1) * YL, :] = turn[pl.ds(r, YL, stride=XROWS), :].astype(BF16)
        mine = pl.ds(pl.multiple_of(py * PIECE, PIECE), PIECE)
        for k in range(1, PY):
            dest = lax.rem(py + k, PY)
            rows = pl.ds(pl.multiple_of(dest * PIECE, PIECE), PIECE)
            a2_c[2 * t, g, k] = send(
                sbuf.at[t, g, rows], rbuf.at[t, g, mine], a2_s.at[2 * t, g, k - 1], a2_r.at[2 * t, g, k - 1], at_py(k)
            )
        rbuf[t, g, mine, :] = sbuf[t, g, mine, :]

    def spectrum(t):
        for g in range(GROUPS):
            for k in range(1, PY):
                a2_c[2 * t, g, k].wait_recv()
        rows = jnp.concatenate([rbuf[t, g] for g in range(GROUPS)], axis=1)
        return dot(tab["my"][...], rows).astype(BF16)

    def spread(hat, which):
        part = slice(which * CH * MODES, (which + 1) * CH * MODES)
        chosen = dot(hat, tab["sel"][part, :]).astype(BF16)
        for b in range(HALF):
            us[b * ROWS : (b + 1) * ROWS, :] = chosen[:, b * 128 : (b + 1) * 128]
        for q in range(2):
            if which:
                ue[q, :, :PATTERN] = dot(us[...], tab["expand"][q, :, WIDE:]).astype(BF16)
            else:
                ue[q] = dot(us[...], tab["expand"][q, :, :WIDE]).astype(BF16)

    def mix(which, collapse):
        def body(n, _):
            q, b = n // HALF, lax.rem(n, HALF)
            re = pl.ds(pl.multiple_of(b * ROWS, ROWS), KY)
            im = pl.ds(pl.multiple_of(b * ROWS + KY, KY), KY)
            for v in range(WIDE // 128):
                cols = slice(v * 128, min((v + 1) * 128, IO))
                size = cols.stop - cols.start
                at = (v % 3) * 128 if which else v * 128
                w_re, w_im = w[q, re, cols].astype(F32), w[q, im, cols].astype(F32)
                u_re, u_im = ue[q, re, at : at + size].astype(F32), ue[q, im, at : at + size].astype(F32)
                if which:
                    prod[q, re, cols] = (w_re * u_re + w_im * u_im).astype(BF16)
                    prod[q, im, cols] = (w_re * u_im - w_im * u_re).astype(BF16)
                else:
                    prod[q, re, cols] = (w_re * u_re - w_im * u_im).astype(BF16)
                    prod[q, im, cols] = (w_re * u_im + w_im * u_re).astype(BF16)
            return 0

        lax.fori_loop(0, MODES, body, 0)
        summed = (dot(prod[0], collapse[0]) + dot(prod[1], collapse[1])).astype(BF16)
        lined = jnp.concatenate([summed[b * ROWS : (b + 1) * ROWS] for b in range(HALF)], axis=1)
        return dot(lined, tab["place"][...]).astype(BF16)

    own_block = pl.ds(pl.multiple_of(px * BLOCK, BLOCK), BLOCK)

    def inverse_send(t, mixed):
        spatial = dot(tab["myt"][...], mixed).astype(BF16)
        mine = pl.ds(pl.multiple_of(px * BLOCK + py * PIECE, PIECE), PIECE)
        for g in range(GROUPS):
            vbuf[t, g] = spatial[:, g * LANES : (g + 1) * LANES]
            for k in range(1, PY):
                dest = lax.rem(py + k, PY)
                rows = pl.ds(pl.multiple_of(dest * PIECE, PIECE), PIECE)
                a2_c[2 * t + 1, g, k] = send(
                    vbuf.at[t, g, rows], ag.at[t, g, mine],
                    a2_s.at[2 * t + 1, g, k - 1], a2_r.at[2 * t + 1, g, k - 1], at_py(k),
                )
            here = pl.ds(pl.multiple_of(py * PIECE, PIECE), PIECE)
            ag[t, g, mine, :] = vbuf[t, g, here, :]

    def gather_send(t, g):
        for k in range(1, PY):
            a2_c[2 * t + 1, g, k].wait_recv()
        for j in (2, 1, 3):
            ag_c[t, g, j] = send(
                ag.at[t, g, own_block], ag.at[t, g, own_block], ag_s.at[t, g, j - 1], ag_r.at[t, g, j - 1], at_px(j)
            )

    def cross_back(t, g):
        for j in range(1, PX):
            ag_c[t, g, j].wait_recv()

        wide_ag[...] = ag[t, g].astype(F32)
        for y in range(YL):
            xbuf[:, y * LANES : (y + 1) * LANES] = wide_ag[pl.ds(y, 2 * KX, stride=YL), :].astype(BF16)
        made = dot(tab["m1t"][...], xbuf[...])
        for y in range(YL):
            back[y * 2 * XL : (y + 1) * 2 * XL, :] = made[:, y * LANES : (y + 1) * LANES]
        for x in range(XL):
            for s in range(2):
                tbuf[x * YL : (x + 1) * YL, s * LANES : (s + 1) * LANES] = back[
                    pl.ds(s * XL + x, YL, stride=2 * XL), :
                ].astype(BF16)

    def field_values(table):
        made = dot(tbuf[...], table[...])
        for c in range(GC):
            zval[c] = made[:, c * NZ : (c + 1) * NZ]

    def bypass_part(matrix, source, first, last):
        def body(b, _):
            parts = []
            for e in range(2):
                rows = pl.ds(pl.multiple_of(b * 32 + e * 16, 16), 16)
                parts.append(source[:, rows, :].reshape(CH * YL, NZ))
            value = dot(matrix[...], jnp.concatenate(parts, axis=1))
            for e in range(2):
                rows = pl.ds(pl.multiple_of(b * 32 + e * 16, 16), 16)
                pb[:, rows, :] = value[:, e * NZ : (e + 1) * NZ].reshape(CH, YL, NZ)
            return 0

        lax.fori_loop(first, last, body, 0)

    def share(name, n, data):
        for j in range(1, 4):
            dp_c[name, j] = send(data.at[0], data.at[j], dp_s.at[n, j], dp_r.at[n, j], at_y(j))
        dp_c[name, 4] = send(data.at[0], data.at[4], dp_s.at[n, 4], dp_r.at[n, 4], far)

    def share_far(name, n, data):
        dp_c[name, 4].wait_recv()
        for j in range(1, 4):
            dp_c[name, 4 + j] = send(data.at[4], data.at[4 + j], dp_s.at[n, 4 + j], dp_r.at[n, 4 + j], at_y(j))

    need("f0", "dz", "m1")
    load("f1", fields_h.at[pl.ds(GC, GC)], fields.at[pl.ds(GC, GC)], 3)
    load("f2", fields_h.at[pl.ds(2 * GC, GC)], fields.at[pl.ds(2 * GC, GC)], 4)
    load("w", w_h, w4, 5)
    load("m1t", tab_h["m1t"].at[px], tab["m1t"], 6)
    for g in range(GROUPS):
        need("f%d" % g)
        if g == GROUPS - 1:
            load_later()

        depth(fields, g, tab["dz"])
        if g == 0:
            pl.semaphore_wait(barrier, len(partners))
        cross_and_send(0, g)

    need("rep", "rept")
    mask = lax.rem(lax.broadcasted_iota(jnp.int32, (CH * YL, CH * YL), 0), YL) == lax.rem(
        lax.broadcasted_iota(jnp.int32, (CH * YL, CH * YL), 1), YL
    )
    left = dot(tab["rep"][...], byp[...]).astype(BF16)
    full = dot(left, tab["rept"][...])
    bypk[...] = jnp.where(mask, full, 0.0).astype(BF16)
    bypkt[...] = jnp.where(mask, full, 0.0).T.astype(BF16)

    need("w")

    def weight_rows(b, _):
        for q in range(2):
            for part in range(2):
                w[q, pl.ds(pl.multiple_of(b * ROWS + part * KY, KY), KY), :] = w4[:, 2 * b + q, part, :]
        return 0

    lax.fori_loop(0, HALF // 2, weight_rows, 0)
    reduce_and_send(0, 0)
    lax.fori_loop(HALF // 2, HALF, weight_rows, 0)
    reduce_and_send(0, 1)
    reduce_and_send(0, 2)

    need("my", "sel", "expand", "sum_o", "place", "myt")
    u_hat = spectrum(0)
    dpu[0] = u_hat
    share("u", 0, dpu)
    spread(u_hat, 0)
    inverse_send(0, mix(0, tab["sum_o"]))
    bypass_part(bypk, fields, 0, 9)
    need("m1t", "dht", "dh", "cot")
    for g in range(GROUPS):
        gather_send(0, g)
    share_far("u", 0, dpu)
    bypass_part(bypk, fields, 9, CELLS // 32)

    for g in range(GROUPS):
        cross_back(0, g)
        field_values(tab["dht"])

        def body(r, _):
            rows = pl.ds(pl.multiple_of(r * CHUNK, CHUNK), CHUNK)
            for c in range(GC):
                pre = zval[c, rows, :] + pb[g * GC + c, rows, :]
                slope = gelu_slope(pre)
                gp[g * GC + c, rows, :] = (cot[g * GC + c, rows, :].astype(F32) * slope).astype(BF16)
            return 0

        lax.fori_loop(0, CELLS // CHUNK, body, 0)
        depth(gp, g, tab["dh"])
        cross_and_send(1, g)
        if g:
            reduce_and_send(1, g - 1)
    bypass_part(bypkt, gp, 0, CELLS // 32)
    reduce_and_send(1, GROUPS - 1)

    need("sum_i", "dzt")
    g_hat = spectrum(1)
    dpg[0] = g_hat
    share("g", 1, dpg)
    spread(g_hat, 1)
    inverse_send(1, mix(1, tab["sum_i"]))

    def choose(h):
        for j in range(NEAR * h, NEAR * (h + 1)):
            if j:
                if h == 0 or j > NEAR:
                    dp_c["u", j].wait_recv()
                    dp_c["g", j].wait_recv()
        part = slice(NEAR * h, NEAR * (h + 1))
        both = jnp.concatenate(
            [dpu[part].reshape(NEAR * ROWS, CH * MODES), dpg[part].reshape(NEAR * ROWS, CH * MODES)], axis=1
        )
        chosen = dot(both, tab["sel"][...]).astype(BF16)
        for b in range(HALF):
            gs[b] = chosen[:, b * 128 : (b + 1) * 128]

    def gw_part(h, first, last):
        def gw_body(b, _):
            for q in range(2):
                wide[...] = dot(gs[b], tab["expand"][q])
                for v in range(WIDE // 128):
                    cols = slice(v * 128, min((v + 1) * 128, IO))
                    size = cols.stop - cols.start
                    at = WIDE + (v % 3) * 128
                    real = acc[2 * b + q, 0, :, cols] if h else None
                    imag = acc[2 * b + q, 1, :, cols] if h else None
                    for d in range(NEAR):
                        re = slice(d * ROWS, d * ROWS + KY)
                        im = slice(d * ROWS + KY, (d + 1) * ROWS)
                        u_re, u_im = wide[re, cols], wide[im, cols]
                        g_re, g_im = wide[re, at : at + size], wide[im, at : at + size]
                        more_real = g_re * u_re + g_im * u_im
                        more_imag = g_im * u_re - g_re * u_im
                        real = more_real if real is None else real + more_real
                        imag = more_imag if imag is None else imag + more_imag
                    if h:
                        gw[:, 2 * b + q, 0, cols] = real
                        gw[:, 2 * b + q, 1, cols] = imag
                    else:
                        acc[2 * b + q, 0, :, cols] = real
                        acc[2 * b + q, 1, :, cols] = imag
            return 0

        lax.fori_loop(first, last, gw_body, 0)

    choose(0)
    gw_part(0, 0, 3)
    gather_send(1, 0)
    share_far("g", 1, dpg)
    gather_send(1, 1)
    gather_send(1, 2)
    gw_part(0, 3, HALF)

    stores = []

    def finish(g):
        cross_back(1, g)
        field_values(tab["dzt"])

        def body(r, _):
            rows = pl.ds(pl.multiple_of(r * CHUNK, CHUNK), CHUNK)
            for c in range(GC):
                out[g * GC + c, rows, :] = (zval[c, rows, :] + pb[g * GC + c, rows, :]).astype(BF16)
            return 0

        lax.fori_loop(0, CELLS // CHUNK, body, 0)
        part = pl.ds(g * GC, GC)
        copy = pltpu.make_async_copy(out.at[part], gf_h.at[part], store_sem.at[g])
        copy.start()
        stores.append(copy)

    finish(0)

    choose(1)
    gw_part(1, 0, HALF)
    stores.append(pltpu.make_async_copy(gw, gw_h, store_sem.at[GROUPS]))
    stores[-1].start()

    finish(1)
    finish(2)

    for copy in stores:
        copy.wait()
    for copy in sends:
        copy.wait_send()


def shards(fields, cotangent, spectral_weight, bypass):
    tab = tables()
    arrays = [jnp.asarray(tab[name]) for name in NAMES]
    any_spec = pl.BlockSpec(memory_space=pl.ANY)
    vmem = pltpu.VMEM
    shapes = [a.shape[1:] if name in ("m1", "m1t") else a.shape for name, a in zip(NAMES, arrays)]
    scratch = [vmem(shape, BF16) for shape in shapes] + [
        vmem((CH, CELLS, NZ), BF16),
        vmem((CH, CELLS, NZ), BF16),
        vmem((CH, CELLS, NZ), BF16),
        vmem((KY, MODES, 2, IO), BF16),
        vmem((2, HALF * ROWS, IO), BF16),
        vmem((CH, CELLS, NZ), F32),
        vmem((CH, CELLS, NZ), BF16),
        vmem((CH * YL, CH * YL), BF16),
        vmem((CH * YL, CH * YL), BF16),
        vmem((2 * XL, YLANES), BF16),
        vmem((CELLS, 2 * LANES), BF16),
        vmem((GC, CELLS, NZ), F32),
        vmem((2, CELLS, LANES), F32),
        vmem((YL * XROWS, LANES), F32),
        vmem((YL * 2 * XL, LANES), F32),
        vmem((2 * KX * YL, LANES), F32),
        vmem((2, GROUPS, PX, XROWS, YLANES), BF16),
        vmem((2, GROUPS, PX - 1, XROWS, YLANES), BF16),
        vmem((2, GROUPS, BLOCK, LANES), BF16),
        vmem((2, GROUPS, BLOCK, LANES), BF16),
        vmem((2, GROUPS, BLOCK, LANES), BF16),
        vmem((2, GROUPS, PX * BLOCK, LANES), BF16),
        vmem((DP, ROWS, CH * MODES), BF16),
        vmem((DP, ROWS, CH * MODES), BF16),
        vmem((2, HALF * ROWS, WIDE), BF16),
        vmem((2, HALF * ROWS, IO), BF16),
        vmem((HALF * ROWS, 128), BF16),
        vmem((HALF, NEAR * ROWS, 128), BF16),
        vmem((NEAR * ROWS, WIDE + PATTERN), F32),
        vmem((MODES, 2, KY, WIDE), F32),
        vmem((KY, MODES, 2, IO), F32),
        pltpu.SemaphoreType.DMA((len(NAMES) + 5,)),
        pltpu.SemaphoreType.DMA((GROUPS + 1,)),
        pltpu.SemaphoreType.DMA((2, GROUPS, PX - 1)),
        pltpu.SemaphoreType.DMA((2, GROUPS, PX - 1)),
        pltpu.SemaphoreType.DMA((4, GROUPS, PY - 1)),
        pltpu.SemaphoreType.DMA((4, GROUPS, PY - 1)),
        pltpu.SemaphoreType.DMA((2, GROUPS, PX - 1)),
        pltpu.SemaphoreType.DMA((2, GROUPS, PX - 1)),
        pltpu.SemaphoreType.DMA((2, DP)),
        pltpu.SemaphoreType.DMA((2, DP)),
    ]
    gw, gf = pl.pallas_call(
        kernel,
        out_shape=(
            jax.ShapeDtypeStruct((KY, MODES, 2, IO), F32),
            jax.ShapeDtypeStruct((CH, CELLS, NZ), BF16),
        ),
        in_specs=[any_spec] * 3 + [pl.BlockSpec(memory_space=pltpu.VMEM)] + [any_spec] * len(arrays),
        out_specs=(any_spec, any_spec),
        scratch_shapes=scratch,
        compiler_params=pltpu.CompilerParams(
            collective_id=0, has_side_effects=True, vmem_limit_bytes=60 * 1024 * 1024
        ),
        cost_estimate=pl.CostEstimate(flops=20_000_000_000, bytes_accessed=30_000_000, transcendentals=3_000_000),
    )(
        fields.reshape(CH, CELLS, NZ), cotangent.reshape(CH, CELLS, NZ), spectral_weight, bypass, *arrays
    )
    return gw, gf.reshape(1, CH, XL, YL, NZ)


def solution(mesh):
    in_specs = (
        P("dp", None, "px", "py", None),
        P("dp", None, "px", "py", None),
        P(("px", "py"), None, None, None),
        P(),
    )
    out_specs = (P(("px", "py"), None, None, None), P("dp", None, "px", "py", None))
    return jax.shard_map(shards, mesh=mesh, in_specs=in_specs, out_specs=out_specs, check_vma=False)
```

```python
import functools
import math

import jax
import jax.numpy as jnp
import ml_dtypes
import numpy as np
from jax import lax
from jax.experimental import pallas as pl
from jax.experimental.pallas import tpu as pltpu
from jax.sharding import PartitionSpec as P

MODES = 16
NX = 128
NY = 128
NZ = 128
CH = 24
PX = 4
PY = 8
DP = 8
XL = NX // PX
YL = NY // PY
CELLS = XL * YL
GROUPS = 3
GC = CH // GROUPS
LANES = GC * MODES
KX = 2 * MODES
KY = 2 * MODES
ROWS = 2 * KY
BLOCK = PY * 2 * YL
PIECE = 2 * YL
IO = CH * CH
WIDE = 640
PATTERN = 384
ORDER = (2, 1, 3, 0)
HALF = MODES // 2
XROWS = 2 * PY
YLANES = YL * LANES
NEAR = DP // 2
CHUNK = 128
MESH = pl.DeviceIdType.MESH
F32 = jnp.float32
BF16 = jnp.bfloat16


def bf(array):
    return np.asarray(array, np.float32).astype(ml_dtypes.bfloat16)


def axis_table(length, mode_count):
    grid_pos = np.arange(length)
    kept_freq = np.concatenate([np.arange(mode_count), np.arange(length - mode_count, length)])
    angles = 2.0 * math.pi * (kept_freq[None, :] * grid_pos[:, None] % length) / length
    norm_scale = length ** (-0.5)
    cosine = np.cos(angles) * norm_scale
    sine_part = np.sin(angles) * norm_scale
    result = np.zeros((2, length, 2, 2 * mode_count))
    result[0, :, 0, :] = cosine
    result[1, :, 0, :] = sine_part
    result[0, :, 1, :] = -sine_part
    result[1, :, 1, :] = cosine
    return result


def depth_tables(length, mode_count):
    grid_pos = np.arange(length)
    frequency = np.arange(mode_count)
    angles = 2.0 * math.pi * (frequency[None, :] * grid_pos[:, None] % length) / length
    norm_scale = length ** (-0.5)
    result = np.zeros((length, mode_count, 2))
    result[:, :, 0] = np.cos(angles) * norm_scale
    result[:, :, 1] = -np.sin(angles) * norm_scale
    doubling = np.where(frequency == 0, 1.0, 2.0)
    return result, result * doubling[None, :, None]


@functools.cache
def tables():
    plain, doubled = depth_tables(NZ, MODES)

    def depth(table):
        out = np.zeros((GC, NZ, 2, GC, MODES))
        for c in range(GC):
            out[c, :, :, c, :] = table.transpose(0, 2, 1)
        return out.reshape(GC * NZ, 2 * LANES)

    dz, dh = depth(plain), depth(doubled)
    cross = axis_table(NX, MODES).reshape(2, PX, XL, 2, KX)
    m1 = cross.transpose(1, 4, 3, 0, 2).reshape(PX, KX * 2, 2 * XL)
    along = axis_table(NY, MODES).reshape(2, PY, YL, 2, KY)
    my = along.transpose(3, 4, 1, 0, 2).reshape(ROWS, BLOCK)
    sel = np.zeros((2, CH, MODES, MODES, 2, 32))
    for c in range(CH):
        for k in range(MODES):
            sel[0, c, k, k, 0, c] = 1.0
            sel[1, c, k, k, 1, c] = 1.0
    sel = sel.reshape(2 * CH * MODES, MODES * 64)
    exp_i = np.zeros((CH, CH, CH))
    exp_o = np.zeros((CH, CH, CH))
    for c in range(CH):
        exp_i[c, c, :] = 1.0
        exp_o[c, :, c] = 1.0
    exp_i = exp_i.reshape(CH, IO)
    exp_o = exp_o.reshape(CH, IO)
    expand = np.zeros((2, 2, 64, WIDE + PATTERN))
    sum_i = np.zeros((2, IO, 2, 64))
    sum_o = np.zeros((2, IO, 2, 64))
    for q in range(2):
        expand[q, q, :CH, :IO] = exp_i
        expand[q, q, 32 : 32 + CH, WIDE:] = exp_o[:, :PATTERN]
        sum_i[q, :, q, :CH] = exp_i.T
        sum_o[q, :, q, :CH] = exp_o.T
    expand = expand.reshape(2, 128, WIDE + PATTERN)
    sum_i = sum_i.reshape(2, IO, 128)
    sum_o = sum_o.reshape(2, IO, 128)
    turned = np.stack([
        m1[p].reshape(PX, XROWS, 2 * XL)[[(p + j) % PX for j in ORDER]].reshape(PX * XROWS, 2 * XL)
        for p in range(PX)
    ])
    rep = np.zeros((CH * YL, CH))
    for c in range(CH):
        rep[c * YL : (c + 1) * YL, c] = 1.0
    return dict(
        dz=bf(dz), dh=bf(dh), dzt=bf(dz.T), dht=bf(dh.T),
        m1=bf(turned), m1t=bf(m1.transpose(0, 2, 1)),
        my=bf(my), myt=bf(my.T), sel=bf(sel), place=bf(sel[: CH * MODES].T),
        expand=bf(expand), sum_i=bf(sum_i), sum_o=bf(sum_o),
        rep=bf(rep), rept=bf(rep.T),
    )


NAMES = (
    "dz", "m1", "m1t", "rep", "rept", "my", "sel", "expand", "sum_o", "place", "myt", "dht", "dh",
    "sum_i", "dzt",
)


def dot(a, b):
    return jnp.dot(a, b, preferred_element_type=F32)


def gelu_slope(values):
    normal_cdf = 0.5 * (1.0 + lax.erf(values * 0.7071067811865476))
    density = jnp.exp(-0.5 * values * values) * 0.3989422804014327
    return normal_cdf + values * density


def group_values(block, m1t, table, wide_ag, xbuf, back, tbuf, zval):
    wide_ag[...] = block.astype(F32)
    for y in range(YL):
        xbuf[:, y * LANES : (y + 1) * LANES] = wide_ag[pl.ds(y, 2 * KX, stride=YL), :].astype(BF16)
    made = dot(m1t[...], xbuf[...])
    for y in range(YL):
        back[y * 2 * XL : (y + 1) * 2 * XL, :] = made[:, y * LANES : (y + 1) * LANES]
    for x in range(XL):
        for s in range(2):
            tbuf[x * YL : (x + 1) * YL, s * LANES : (s + 1) * LANES] = back[
                pl.ds(s * XL + x, YL, stride=2 * XL), :
            ].astype(BF16)
    made = dot(tbuf[...], table[...])
    for c in range(GC):
        zval[c] = made[:, c * NZ : (c + 1) * NZ]


def add_bypass(zval, bypass_values, out, first, last):
    def body(r, _):
        rows = pl.ds(pl.multiple_of(r * CHUNK, CHUNK), CHUNK)
        for c in range(GC):
            out[c, rows, :] = (zval[c, rows, :] + bypass_values[c, rows, :].astype(F32)).astype(BF16)
        return 0

    lax.fori_loop(first, last, body, 0)


def kernel(*refs):
    fields_h, cot_h, w_h, byp = refs[:4]
    tab_h = dict(zip(NAMES, refs[4 : 4 + len(NAMES)]))
    refs = refs[4 + len(NAMES) :]
    gw_h, gf_h, ag_h, pb_h = refs[:4]
    refs = refs[4:]
    tab = dict(zip(NAMES, refs[: len(NAMES)]))
    (
        fields, cot, gp, w4, w, pb, pb16, out, bypk, bypkt, xbuf, tbuf, zval, lines, turn, back, wide_ag, ybuf, rs, sbuf, rbuf, vbuf, ag, dpu, dpg,
        ue, prod, us, gs, wide, acc, gw,
        load_sem, store_sem, rs_s, rs_r, a2_s, a2_r, ag_s, ag_r, dp_s, dp_r,
    ) = refs[len(NAMES) :]

    px = lax.axis_index("px")
    py = lax.axis_index("py")
    dp = lax.axis_index("dp")
    zhi = dp // 4
    yy = lax.rem(dp, 4)

    loads = {}

    def load(name, src, dst, index):
        copy = pltpu.make_async_copy(src, dst, load_sem.at[index])
        copy.start()
        loads[name] = copy

    def load_later():
        for index, name in enumerate(NAMES[3:]):
            load(name, tab_h[name], tab[name], 7 + index)
        load("cot", cot_h, cot, 7 + len(NAMES) - 3)

    load("f0", fields_h.at[pl.ds(0, GC)], fields.at[pl.ds(0, GC)], 0)
    load("dz", tab_h["dz"], tab["dz"], 1)
    load("m1", tab_h["m1"].at[px], tab["m1"], 2)
    waited = set()

    def need(*names):
        for name in names:
            if name not in waited:
                loads[name].wait()
                waited.add(name)

    def at_px(j):
        return {"px": lax.rem(px + j, PX)}

    def at_py(k):
        return {"py": lax.rem(py + k, PY)}

    def at_y(j):
        return {"dp": zhi * 4 + lax.rem(yy + j, 4)}

    far = {"dp": lax.rem(dp + 4, DP)}
    partners = [at_px(j) for j in range(1, PX)] + [at_py(k) for k in range(1, PY)]
    partners += [at_y(j) for j in range(1, 4)] + [far]
    barrier = pltpu.get_barrier_semaphore()
    for where in partners:
        pl.semaphore_signal(barrier, inc=1, device_id=where, device_id_type=MESH)

    sends = []

    def send(src, dst, send_sem, recv_sem, where):
        copy = pltpu.make_async_remote_copy(
            src_ref=src, dst_ref=dst, send_sem=send_sem, recv_sem=recv_sem,
            device_id=where, device_id_type=MESH,
        )
        copy.start()
        sends.append(copy)
        return copy

    rs_c, a2_c, ag_c, dp_c = {}, {}, {}, {}

    def cross_and_send(t, g):
        made = dot(tab["m1"][...], xbuf[...]).astype(BF16)
        for pos, j in enumerate(ORDER):
            ybuf[t, g, pos] = made[pos * XROWS : (pos + 1) * XROWS]
            if j:
                rs_c[t, g, j] = send(
                    ybuf.at[t, g, pos], rs.at[t, g, j - 1], rs_s.at[t, g, j - 1], rs_r.at[t, g, j - 1], at_px(j)
                )

    def depth(source, g, table):
        lhs = jnp.concatenate([source[g * GC + c] for c in range(GC)], axis=1)
        part = dot(lhs, table[...])
        for s in range(2):
            lines[s] = part[:, s * LANES : (s + 1) * LANES]
        for y in range(YL):
            for s in range(2):
                xbuf[s * XL : (s + 1) * XL, y * LANES : (y + 1) * LANES] = lines[
                    s, pl.ds(y, XL, stride=YL), :
                ].astype(BF16)

    def reduce_and_send(t, g):
        for j in range(1, PX):
            rs_c[t, g, j].wait_recv()
        total = ybuf[t, g, ORDER.index(0)].astype(F32)
        for j in range(1, PX):
            total = total + rs[t, g, j - 1].astype(F32)
        for y in range(YL):
            turn[y * XROWS : (y + 1) * XROWS, :] = total[:, y * LANES : (y + 1) * LANES]
        for r in range(XROWS):
            sbuf[t, g, r * YL : (r + 1) * YL, :] = turn[pl.ds(r, YL, stride=XROWS), :].astype(BF16)
        mine = pl.ds(pl.multiple_of(py * PIECE, PIECE), PIECE)
        for k in range(1, PY):
            dest = lax.rem(py + k, PY)
            rows = pl.ds(pl.multiple_of(dest * PIECE, PIECE), PIECE)
            a2_c[2 * t, g, k] = send(
                sbuf.at[t, g, rows], rbuf.at[t, g, mine], a2_s.at[2 * t, g, k - 1], a2_r.at[2 * t, g, k - 1], at_py(k)
            )
        rbuf[t, g, mine, :] = sbuf[t, g, mine, :]

    def spectrum(t):
        for g in range(GROUPS):
            for k in range(1, PY):
                a2_c[2 * t, g, k].wait_recv()
        rows = jnp.concatenate([rbuf[t, g] for g in range(GROUPS)], axis=1)
        return dot(tab["my"][...], rows).astype(BF16)

    def spread(hat, which):
        part = slice(which * CH * MODES, (which + 1) * CH * MODES)
        chosen = dot(hat, tab["sel"][part, :]).astype(BF16)
        for b in range(HALF):
            us[b * ROWS : (b + 1) * ROWS, :] = chosen[:, b * 128 : (b + 1) * 128]
        for q in range(2):
            if which:
                ue[q, :, :PATTERN] = dot(us[...], tab["expand"][q, :, WIDE:]).astype(BF16)
            else:
                ue[q] = dot(us[...], tab["expand"][q, :, :WIDE]).astype(BF16)

    def mix(which, collapse):
        def body(n, _):
            q, b = n // HALF, lax.rem(n, HALF)
            re = pl.ds(pl.multiple_of(b * ROWS, ROWS), KY)
            im = pl.ds(pl.multiple_of(b * ROWS + KY, KY), KY)
            for v in range(WIDE // 128):
                cols = slice(v * 128, min((v + 1) * 128, IO))
                size = cols.stop - cols.start
                at = (v % 3) * 128 if which else v * 128
                w_re, w_im = w[q, re, cols].astype(F32), w[q, im, cols].astype(F32)
                u_re, u_im = ue[q, re, at : at + size].astype(F32), ue[q, im, at : at + size].astype(F32)
                if which:
                    prod[q, re, cols] = (w_re * u_re + w_im * u_im).astype(BF16)
                    prod[q, im, cols] = (w_re * u_im - w_im * u_re).astype(BF16)
                else:
                    prod[q, re, cols] = (w_re * u_re - w_im * u_im).astype(BF16)
                    prod[q, im, cols] = (w_re * u_im + w_im * u_re).astype(BF16)
            return 0

        lax.fori_loop(0, MODES, body, 0)
        summed = (dot(prod[0], collapse[0]) + dot(prod[1], collapse[1])).astype(BF16)
        lined = jnp.concatenate([summed[b * ROWS : (b + 1) * ROWS] for b in range(HALF)], axis=1)
        return dot(lined, tab["place"][...]).astype(BF16)

    own_block = pl.ds(pl.multiple_of(px * BLOCK, BLOCK), BLOCK)

    def inverse_send(t, mixed):
        spatial = dot(tab["myt"][...], mixed).astype(BF16)
        mine = pl.ds(pl.multiple_of(px * BLOCK + py * PIECE, PIECE), PIECE)
        for g in range(GROUPS):
            vbuf[t, g] = spatial[:, g * LANES : (g + 1) * LANES]
            for k in range(1, PY):
                dest = lax.rem(py + k, PY)
                rows = pl.ds(pl.multiple_of(dest * PIECE, PIECE), PIECE)
                a2_c[2 * t + 1, g, k] = send(
                    vbuf.at[t, g, rows], ag.at[t, g, mine],
                    a2_s.at[2 * t + 1, g, k - 1], a2_r.at[2 * t + 1, g, k - 1], at_py(k),
                )
            here = pl.ds(pl.multiple_of(py * PIECE, PIECE), PIECE)
            ag[t, g, mine, :] = vbuf[t, g, here, :]

    def gather_send(t, g):
        for k in range(1, PY):
            a2_c[2 * t + 1, g, k].wait_recv()
        for j in (2, 1, 3):
            ag_c[t, g, j] = send(
                ag.at[t, g, own_block], ag.at[t, g, own_block], ag_s.at[t, g, j - 1], ag_r.at[t, g, j - 1], at_px(j)
            )

    def cross_back(t, g):
        for j in range(1, PX):
            ag_c[t, g, j].wait_recv()

        group_values(
            ag[t, g], tab["m1t"], tab["dht" if t == 0 else "dzt"], wide_ag, xbuf, back, tbuf, zval
        )

    def bypass_part(matrix, source, target, first, last):
        def body(b, _):
            parts = []
            for e in range(2):
                rows = pl.ds(pl.multiple_of(b * 32 + e * 16, 16), 16)
                parts.append(source[:, rows, :].reshape(CH * YL, NZ))
            value = dot(matrix[...], jnp.concatenate(parts, axis=1))
            for e in range(2):
                rows = pl.ds(pl.multiple_of(b * 32 + e * 16, 16), 16)
                target[:, rows, :] = value[:, e * NZ : (e + 1) * NZ].reshape(CH, YL, NZ).astype(target.dtype)
            return 0

        lax.fori_loop(first, last, body, 0)

    def share(name, n, data):
        for j in range(1, 4):
            dp_c[name, j] = send(data.at[0], data.at[j], dp_s.at[n, j], dp_r.at[n, j], at_y(j))
        dp_c[name, 4] = send(data.at[0], data.at[4], dp_s.at[n, 4], dp_r.at[n, 4], far)

    def share_far(name, n, data):
        dp_c[name, 4].wait_recv()
        for j in range(1, 4):
            dp_c[name, 4 + j] = send(data.at[4], data.at[4 + j], dp_s.at[n, 4 + j], dp_r.at[n, 4 + j], at_y(j))

    need("f0", "dz", "m1")
    load("f1", fields_h.at[pl.ds(GC, GC)], fields.at[pl.ds(GC, GC)], 3)
    load("f2", fields_h.at[pl.ds(2 * GC, GC)], fields.at[pl.ds(2 * GC, GC)], 4)
    load("w", w_h, w4, 5)
    load("m1t", tab_h["m1t"].at[px], tab["m1t"], 6)
    for g in range(GROUPS):
        need("f%d" % g)
        if g == GROUPS - 1:
            load_later()

        depth(fields, g, tab["dz"])
        if g == 0:
            pl.semaphore_wait(barrier, len(partners))
        cross_and_send(0, g)

    need("rep", "rept")
    mask = lax.rem(lax.broadcasted_iota(jnp.int32, (CH * YL, CH * YL), 0), YL) == lax.rem(
        lax.broadcasted_iota(jnp.int32, (CH * YL, CH * YL), 1), YL
    )
    left = dot(tab["rep"][...], byp[...]).astype(BF16)
    full = dot(left, tab["rept"][...])
    bypk[...] = jnp.where(mask, full, 0.0).astype(BF16)
    bypkt[...] = jnp.where(mask, full, 0.0).T.astype(BF16)

    need("w")

    def weight_rows(b, _):
        for q in range(2):
            for part in range(2):
                w[q, pl.ds(pl.multiple_of(b * ROWS + part * KY, KY), KY), :] = w4[:, 2 * b + q, part, :]
        return 0

    lax.fori_loop(0, HALF // 2, weight_rows, 0)
    reduce_and_send(0, 0)
    lax.fori_loop(HALF // 2, HALF, weight_rows, 0)
    reduce_and_send(0, 1)
    reduce_and_send(0, 2)

    need("my", "sel", "expand", "sum_o", "place", "myt")
    u_hat = spectrum(0)
    dpu[0] = u_hat
    share("u", 0, dpu)
    spread(u_hat, 0)
    inverse_send(0, mix(0, tab["sum_o"]))
    bypass_part(bypk, fields, pb, 0, 9)
    need("m1t", "dht", "dh", "cot")
    for g in range(GROUPS):
        gather_send(0, g)
    share_far("u", 0, dpu)
    bypass_part(bypk, fields, pb, 9, CELLS // 32)

    for g in range(GROUPS):
        cross_back(0, g)

        def body(r, _):
            rows = pl.ds(pl.multiple_of(r * CHUNK, CHUNK), CHUNK)
            for c in range(GC):
                pre = zval[c, rows, :] + pb[g * GC + c, rows, :]
                slope = gelu_slope(pre)
                gp[g * GC + c, rows, :] = (cot[g * GC + c, rows, :].astype(F32) * slope).astype(BF16)
            return 0

        lax.fori_loop(0, CELLS // CHUNK, body, 0)
        depth(gp, g, tab["dh"])
        cross_and_send(1, g)
        if g:
            reduce_and_send(1, g - 1)
    bypass_part(bypkt, gp, pb16, 0, CELLS // 32)
    stores = [pltpu.make_async_copy(pb16.at[pl.ds(GC, 2 * GC)], pb_h, store_sem.at[0])]
    stores[0].start()
    reduce_and_send(1, GROUPS - 1)

    need("sum_i", "dzt")
    g_hat = spectrum(1)
    dpg[0] = g_hat
    share("g", 1, dpg)
    spread(g_hat, 1)
    inverse_send(1, mix(1, tab["sum_i"]))

    def choose(h):
        for j in range(NEAR * h, NEAR * (h + 1)):
            if j:
                if h == 0 or j > NEAR:
                    dp_c["u", j].wait_recv()
                    dp_c["g", j].wait_recv()
        part = slice(NEAR * h, NEAR * (h + 1))
        both = jnp.concatenate(
            [dpu[part].reshape(NEAR * ROWS, CH * MODES), dpg[part].reshape(NEAR * ROWS, CH * MODES)], axis=1
        )
        chosen = dot(both, tab["sel"][...]).astype(BF16)
        for b in range(HALF):
            gs[b] = chosen[:, b * 128 : (b + 1) * 128]

    def gw_part(h, first, last):
        def gw_body(b, _):
            for q in range(2):
                wide[...] = dot(gs[b], tab["expand"][q])
                for v in range(WIDE // 128):
                    cols = slice(v * 128, min((v + 1) * 128, IO))
                    size = cols.stop - cols.start
                    at = WIDE + (v % 3) * 128
                    real = acc[2 * b + q, 0, :, cols] if h else None
                    imag = acc[2 * b + q, 1, :, cols] if h else None
                    for d in range(NEAR):
                        re = slice(d * ROWS, d * ROWS + KY)
                        im = slice(d * ROWS + KY, (d + 1) * ROWS)
                        u_re, u_im = wide[re, cols], wide[im, cols]
                        g_re, g_im = wide[re, at : at + size], wide[im, at : at + size]
                        more_real = g_re * u_re + g_im * u_im
                        more_imag = g_im * u_re - g_re * u_im
                        real = more_real if real is None else real + more_real
                        imag = more_imag if imag is None else imag + more_imag
                    if h:
                        gw[:, 2 * b + q, 0, cols] = real
                        gw[:, 2 * b + q, 1, cols] = imag
                    else:
                        acc[2 * b + q, 0, :, cols] = real
                        acc[2 * b + q, 1, :, cols] = imag
            return 0

        lax.fori_loop(first, last, gw_body, 0)

    choose(0)
    gw_part(0, 0, 3)
    gather_send(1, 0)
    share_far("g", 1, dpg)
    gw_part(0, 3, 5)
    gather_send(1, 1)
    gather_send(1, 2)
    gw_part(0, 5, HALF)

    cross_back(1, 0)
    for h in range(2):
        add_bypass(zval, pb16, out, h * CELLS // CHUNK // 2, (h + 1) * CELLS // CHUNK // 2)
        part = (slice(None), pl.ds(h * CELLS // 2, CELLS // 2))
        stores.append(pltpu.make_async_copy(out.at[part], gf_h.at[part], store_sem.at[1 + h]))
        stores[-1].start()

    choose(1)
    gw_part(1, 0, HALF)
    stores.append(pltpu.make_async_copy(gw, gw_h, store_sem.at[3]))
    stores[-1].start()
    for g in range(1, GROUPS):
        for j in range(1, PX):
            ag_c[1, g, j].wait_recv()
        stores.append(pltpu.make_async_copy(ag.at[1, g], ag_h.at[g - 1], store_sem.at[3 + g]))
        stores[-1].start()

    for copy in stores:
        copy.wait()
    for copy in sends:
        copy.wait_send()


def last_groups(gw_in, gf_in, ag_in, pb_in, m1t_h, dzt_h, gw_out, gf_out,
                gw, gf, ag, pb, m1t, dzt, wide_ag, xbuf, back, tbuf, zval, sem, out_sem):
    px = lax.axis_index("px")
    pairs = [
        (ag_in.at[0], ag.at[0]), (m1t_h.at[px], m1t), (dzt_h, dzt),
        (pb_in.at[pl.ds(0, GC)], pb.at[pl.ds(0, GC)]), (gw_in, gw), (ag_in.at[1], ag.at[1]),
        (pb_in.at[pl.ds(GC, GC)], pb.at[pl.ds(GC, GC)]), (gf_in, gf.at[pl.ds(0, GC)]),
    ]
    reads = [pltpu.make_async_copy(src, dst, sem.at[n]) for n, (src, dst) in enumerate(pairs)]
    for read in reads:
        read.start()
    writes = []

    def write(src, dst):
        writes.append(pltpu.make_async_copy(src, dst, out_sem.at[len(writes)]))
        writes[-1].start()

    for n in range(3):
        reads[n].wait()
    for g in range(1, GROUPS):
        if g == 2:
            reads[5].wait()
        group_values(ag[g - 1], m1t, dzt, wide_ag, xbuf, back, tbuf, zval)
        reads[3 if g == 1 else 6].wait()
        part = pl.ds(g * GC, GC)
        if g == 1:
            reads[4].wait()
            write(gw, gw_out)
        for h in range(2):
            add_bypass(
                zval, pb.at[pl.ds((g - 1) * GC, GC)], gf.at[part],
                h * CELLS // CHUNK // 2, (h + 1) * CELLS // CHUNK // 2,
            )
            rows = pl.ds(h * CELLS // 2, CELLS // 2)
            write(gf.at[part, rows], gf_out.at[part, rows])
        if g == 1:
            reads[7].wait()
            write(gf.at[pl.ds(0, GC)], gf_out.at[pl.ds(0, GC)])
    for copy in writes:
        copy.wait()


def shards(fields, cotangent, spectral_weight, bypass):
    tab = tables()
    arrays = [jnp.asarray(tab[name]) for name in NAMES]
    any_spec = pl.BlockSpec(memory_space=pl.ANY)
    vmem = pltpu.VMEM
    shapes = [a.shape[1:] if name in ("m1", "m1t") else a.shape for name, a in zip(NAMES, arrays)]
    scratch = [vmem(shape, BF16) for shape in shapes] + [
        vmem((CH, CELLS, NZ), BF16),
        vmem((CH, CELLS, NZ), BF16),
        vmem((CH, CELLS, NZ), BF16),
        vmem((KY, MODES, 2, IO), BF16),
        vmem((2, HALF * ROWS, IO), BF16),
        vmem((CH, CELLS, NZ), F32),
        vmem((CH, CELLS, NZ), BF16),
        vmem((GC, CELLS, NZ), BF16),
        vmem((CH * YL, CH * YL), BF16),
        vmem((CH * YL, CH * YL), BF16),
        vmem((2 * XL, YLANES), BF16),
        vmem((CELLS, 2 * LANES), BF16),
        vmem((GC, CELLS, NZ), F32),
        vmem((2, CELLS, LANES), F32),
        vmem((YL * XROWS, LANES), F32),
        vmem((YL * 2 * XL, LANES), F32),
        vmem((2 * KX * YL, LANES), F32),
        vmem((2, GROUPS, PX, XROWS, YLANES), BF16),
        vmem((2, GROUPS, PX - 1, XROWS, YLANES), BF16),
        vmem((2, GROUPS, BLOCK, LANES), BF16),
        vmem((2, GROUPS, BLOCK, LANES), BF16),
        vmem((2, GROUPS, BLOCK, LANES), BF16),
        vmem((2, GROUPS, PX * BLOCK, LANES), BF16),
        vmem((DP, ROWS, CH * MODES), BF16),
        vmem((DP, ROWS, CH * MODES), BF16),
        vmem((2, HALF * ROWS, WIDE), BF16),
        vmem((2, HALF * ROWS, IO), BF16),
        vmem((HALF * ROWS, 128), BF16),
        vmem((HALF, NEAR * ROWS, 128), BF16),
        vmem((NEAR * ROWS, WIDE + PATTERN), F32),
        vmem((MODES, 2, KY, WIDE), F32),
        vmem((KY, MODES, 2, IO), F32),
        pltpu.SemaphoreType.DMA((len(NAMES) + 5,)),
        pltpu.SemaphoreType.DMA((6,)),
        pltpu.SemaphoreType.DMA((2, GROUPS, PX - 1)),
        pltpu.SemaphoreType.DMA((2, GROUPS, PX - 1)),
        pltpu.SemaphoreType.DMA((4, GROUPS, PY - 1)),
        pltpu.SemaphoreType.DMA((4, GROUPS, PY - 1)),
        pltpu.SemaphoreType.DMA((2, GROUPS, PX - 1)),
        pltpu.SemaphoreType.DMA((2, GROUPS, PX - 1)),
        pltpu.SemaphoreType.DMA((2, DP)),
        pltpu.SemaphoreType.DMA((2, DP)),
    ]
    gw, gf, ag, pb = pl.pallas_call(
        kernel,
        out_shape=(
            jax.ShapeDtypeStruct((KY, MODES, 2, IO), F32),
            jax.ShapeDtypeStruct((GC, CELLS, NZ), BF16),
            jax.ShapeDtypeStruct((2, PX * BLOCK, LANES), BF16),
            jax.ShapeDtypeStruct((2 * GC, CELLS, NZ), BF16),
        ),
        in_specs=[any_spec] * 3 + [pl.BlockSpec(memory_space=pltpu.VMEM)] + [any_spec] * len(arrays),
        out_specs=(any_spec,) * 4,
        scratch_shapes=scratch,
        compiler_params=pltpu.CompilerParams(
            collective_id=0, has_side_effects=True, vmem_limit_bytes=60 * 1024 * 1024
        ),
        cost_estimate=pl.CostEstimate(flops=20_000_000_000, bytes_accessed=30_000_000, transcendentals=3_000_000),
    )(
        fields.reshape(CH, CELLS, NZ), cotangent.reshape(CH, CELLS, NZ), spectral_weight, bypass, *arrays
    )
    gw, gf = pl.pallas_call(
        last_groups,
        out_shape=(
            jax.ShapeDtypeStruct((KY, MODES, 2, IO), F32),
            jax.ShapeDtypeStruct((CH, CELLS, NZ), BF16),
        ),
        in_specs=[any_spec] * 6,
        out_specs=(any_spec, any_spec),
        scratch_shapes=[
            vmem((KY, MODES, 2, IO), F32),
            vmem((CH, CELLS, NZ), BF16),
            vmem((2, PX * BLOCK, LANES), BF16),
            vmem((2 * GC, CELLS, NZ), BF16),
            vmem((2 * XL, 2 * KX), BF16),
            vmem((2 * LANES, GC * NZ), BF16),
            vmem((2 * KX * YL, LANES), F32),
            vmem((2 * XL, YLANES), BF16),
            vmem((YL * 2 * XL, LANES), F32),
            vmem((CELLS, 2 * LANES), BF16),
            vmem((GC, CELLS, NZ), F32),
            pltpu.SemaphoreType.DMA((8,)),
            pltpu.SemaphoreType.DMA((6,)),
        ],
        compiler_params=pltpu.CompilerParams(vmem_limit_bytes=56 * 1024 * 1024),
        cost_estimate=pl.CostEstimate(flops=1_000_000_000, bytes_accessed=12_000_000, transcendentals=0),
    )(gw, gf, ag, pb, jnp.asarray(tab["m1t"]), jnp.asarray(tab["dzt"]))
    return gw, gf.reshape(1, CH, XL, YL, NZ)


def solution(mesh):
    in_specs = (
        P("dp", None, "px", "py", None),
        P("dp", None, "px", "py", None),
        P(("px", "py"), None, None, None),
        P(),
    )
    out_specs = (P(("px", "py"), None, None, None), P("dp", None, "px", "py", None))
    return jax.shard_map(shards, mesh=mesh, in_specs=in_specs, out_specs=out_specs, check_vma=False)
```

```python
import functools
import math

import jax
import jax.numpy as jnp
import ml_dtypes
import numpy as np
from jax import lax
from jax.experimental import pallas as pl
from jax.experimental.pallas import tpu as pltpu
from jax.sharding import PartitionSpec as P

MODES = 16
NX = 128
NY = 128
NZ = 128
CH = 24
PX = 4
PY = 8
DP = 8
XL = NX // PX
YL = NY // PY
CELLS = XL * YL
GROUPS = 3
GC = CH // GROUPS
LANES = GC * MODES
KX = 2 * MODES
KY = 2 * MODES
ROWS = 2 * KY
BLOCK = PY * 2 * YL
PIECE = 2 * YL
IO = CH * CH
WIDE = 640
PATTERN = 384
ORDER = (2, 1, 3, 0)
HALF = MODES // 2
XROWS = 2 * PY
YLANES = YL * LANES
NEAR = DP // 2
CHUNK = 128
MESH = pl.DeviceIdType.MESH
F32 = jnp.float32
BF16 = jnp.bfloat16


def bf(array):
    return np.asarray(array, np.float32).astype(ml_dtypes.bfloat16)


def axis_table(length, mode_count):
    grid_pos = np.arange(length)
    kept_freq = np.concatenate([np.arange(mode_count), np.arange(length - mode_count, length)])
    angles = 2.0 * math.pi * (kept_freq[None, :] * grid_pos[:, None] % length) / length
    norm_scale = length ** (-0.5)
    cosine = np.cos(angles) * norm_scale
    sine_part = np.sin(angles) * norm_scale
    result = np.zeros((2, length, 2, 2 * mode_count))
    result[0, :, 0, :] = cosine
    result[1, :, 0, :] = sine_part
    result[0, :, 1, :] = -sine_part
    result[1, :, 1, :] = cosine
    return result


def depth_tables(length, mode_count):
    grid_pos = np.arange(length)
    frequency = np.arange(mode_count)
    angles = 2.0 * math.pi * (frequency[None, :] * grid_pos[:, None] % length) / length
    norm_scale = length ** (-0.5)
    result = np.zeros((length, mode_count, 2))
    result[:, :, 0] = np.cos(angles) * norm_scale
    result[:, :, 1] = -np.sin(angles) * norm_scale
    doubling = np.where(frequency == 0, 1.0, 2.0)
    return result, result * doubling[None, :, None]


@functools.cache
def tables():
    plain, doubled = depth_tables(NZ, MODES)

    def depth(table):
        out = np.zeros((GC, NZ, 2, GC, MODES))
        for c in range(GC):
            out[c, :, :, c, :] = table.transpose(0, 2, 1)
        return out.reshape(GC * NZ, 2 * LANES)

    dz, dh = depth(plain), depth(doubled)
    cross = axis_table(NX, MODES).reshape(2, PX, XL, 2, KX)
    m1 = cross.transpose(1, 4, 3, 0, 2).reshape(PX, KX * 2, 2 * XL)
    along = axis_table(NY, MODES).reshape(2, PY, YL, 2, KY)
    my = along.transpose(3, 4, 1, 0, 2).reshape(ROWS, BLOCK)
    sel = np.zeros((2, CH, MODES, MODES, 2, 32))
    for c in range(CH):
        for k in range(MODES):
            sel[0, c, k, k, 0, c] = 1.0
            sel[1, c, k, k, 1, c] = 1.0
    sel = sel.reshape(2 * CH * MODES, MODES * 64)
    exp_i = np.zeros((CH, CH, CH))
    exp_o = np.zeros((CH, CH, CH))
    for c in range(CH):
        exp_i[c, c, :] = 1.0
        exp_o[c, :, c] = 1.0
    exp_i = exp_i.reshape(CH, IO)
    exp_o = exp_o.reshape(CH, IO)
    expand = np.zeros((2, 2, 64, WIDE + PATTERN))
    sum_i = np.zeros((2, IO, 2, 64))
    sum_o = np.zeros((2, IO, 2, 64))
    for q in range(2):
        expand[q, q, :CH, :IO] = exp_i
        expand[q, q, 32 : 32 + CH, WIDE:] = exp_o[:, :PATTERN]
        sum_i[q, :, q, :CH] = exp_i.T
        sum_o[q, :, q, :CH] = exp_o.T
    expand = expand.reshape(2, 128, WIDE + PATTERN)
    sum_i = sum_i.reshape(2, IO, 128)
    sum_o = sum_o.reshape(2, IO, 128)
    turned = np.stack([
        m1[p].reshape(PX, XROWS, 2 * XL)[[(p + j) % PX for j in ORDER]].reshape(PX * XROWS, 2 * XL)
        for p in range(PX)
    ])
    rep = np.zeros((CH * YL, CH))
    for c in range(CH):
        rep[c * YL : (c + 1) * YL, c] = 1.0
    return dict(
        dz=bf(dz), dh=bf(dh), dzt=bf(dz.T), dht=bf(dh.T),
        m1=bf(turned), m1t=bf(m1.transpose(0, 2, 1)),
        my=bf(my), myt=bf(my.T), sel=bf(sel), place=bf(sel[: CH * MODES].T),
        expand=bf(expand), sum_i=bf(sum_i), sum_o=bf(sum_o),
        rep=bf(rep), rept=bf(rep.T),
    )


NAMES = (
    "dz", "m1", "m1t", "rep", "rept", "my", "sel", "expand", "sum_o", "place", "myt", "dht", "dh",
    "sum_i", "dzt",
)


def dot(a, b):
    return jnp.dot(a, b, preferred_element_type=F32)


def gelu_slope(values):
    normal_cdf = 0.5 * (1.0 + lax.erf(values * 0.7071067811865476))
    density = jnp.exp(-0.5 * values * values) * 0.3989422804014327
    return normal_cdf + values * density


def group_values(block, m1t, table, wide_ag, xbuf, back, tbuf, zval):
    wide_ag[...] = block.astype(F32)
    for y in range(YL):
        xbuf[:, y * LANES : (y + 1) * LANES] = wide_ag[pl.ds(y, 2 * KX, stride=YL), :].astype(BF16)
    made = dot(m1t[...], xbuf[...])
    for y in range(YL):
        back[y * 2 * XL : (y + 1) * 2 * XL, :] = made[:, y * LANES : (y + 1) * LANES]
    for x in range(XL):
        for s in range(2):
            tbuf[x * YL : (x + 1) * YL, s * LANES : (s + 1) * LANES] = back[
                pl.ds(s * XL + x, YL, stride=2 * XL), :
            ].astype(BF16)
    made = dot(tbuf[...], table[...])
    for c in range(GC):
        zval[c] = made[:, c * NZ : (c + 1) * NZ]


def add_bypass(zval, bypass_values, out, first, last):
    def body(r, _):
        rows = pl.ds(pl.multiple_of(r * CHUNK, CHUNK), CHUNK)
        for c in range(GC):
            out[c, rows, :] = (zval[c, rows, :] + bypass_values[c, rows, :].astype(F32)).astype(BF16)
        return 0

    lax.fori_loop(first, last, body, 0)


def kernel(*refs):
    fields_h, cot_h, w_h, byp = refs[:4]
    tab_h = dict(zip(NAMES, refs[4 : 4 + len(NAMES)]))
    refs = refs[4 + len(NAMES) :]
    gw_h, gf_h, ag_h, pb_h = refs[:4]
    refs = refs[4:]
    tab = dict(zip(NAMES, refs[: len(NAMES)]))
    (
        fields, cot, gp, w4, w, pb, pb16, out, bypk, bypkt, xbuf, tbuf, zval, lines, turn, back, wide_ag, ybuf, rs, sbuf, rbuf, vbuf, ag, dpu, dpg,
        ue, prod, us, gs, wide, acc, gw,
        load_sem, store_sem, rs_s, rs_r, a2_s, a2_r, ag_s, ag_r, dp_s, dp_r,
    ) = refs[len(NAMES) :]

    px = lax.axis_index("px")
    py = lax.axis_index("py")
    dp = lax.axis_index("dp")
    zhi = dp // 4
    yy = lax.rem(dp, 4)

    loads = {}

    def load(name, src, dst, index):
        copy = pltpu.make_async_copy(src, dst, load_sem.at[index])
        copy.start()
        loads[name] = copy

    def load_later():
        for index, name in enumerate(NAMES[3:]):
            load(name, tab_h[name], tab[name], 7 + index)
        load("cot", cot_h, cot, 7 + len(NAMES) - 3)

    load("f0", fields_h.at[pl.ds(0, GC)], fields.at[pl.ds(0, GC)], 0)
    load("dz", tab_h["dz"], tab["dz"], 1)
    load("m1", tab_h["m1"].at[px], tab["m1"], 2)
    waited = set()

    def need(*names):
        for name in names:
            if name not in waited:
                loads[name].wait()
                waited.add(name)

    def at_px(j):
        return {"px": lax.rem(px + j, PX)}

    def at_py(k):
        return {"py": lax.rem(py + k, PY)}

    def at_y(j):
        return {"dp": zhi * 4 + lax.rem(yy + j, 4)}

    far = {"dp": lax.rem(dp + 4, DP)}
    partners = [at_px(j) for j in range(1, PX)] + [at_py(k) for k in range(1, PY)]
    partners += [at_y(j) for j in range(1, 4)] + [far]
    barrier = pltpu.get_barrier_semaphore()
    for where in partners:
        pl.semaphore_signal(barrier, inc=1, device_id=where, device_id_type=MESH)

    sends = []

    def send(src, dst, send_sem, recv_sem, where):
        copy = pltpu.make_async_remote_copy(
            src_ref=src, dst_ref=dst, send_sem=send_sem, recv_sem=recv_sem,
            device_id=where, device_id_type=MESH,
        )
        copy.start()
        sends.append(copy)
        return copy

    rs_c, a2_c, ag_c, dp_c = {}, {}, {}, {}

    def cross_and_send(t, g):
        made = dot(tab["m1"][...], xbuf[...]).astype(BF16)
        for pos, j in enumerate(ORDER):
            ybuf[t, g, pos] = made[pos * XROWS : (pos + 1) * XROWS]
            if j:
                rs_c[t, g, j] = send(
                    ybuf.at[t, g, pos], rs.at[t, g, j - 1], rs_s.at[t, g, j - 1], rs_r.at[t, g, j - 1], at_px(j)
                )

    def depth(source, g, table):
        lhs = jnp.concatenate([source[g * GC + c] for c in range(GC)], axis=1)
        part = dot(lhs, table[...])
        for s in range(2):
            lines[s] = part[:, s * LANES : (s + 1) * LANES]
        for y in range(YL):
            for s in range(2):
                xbuf[s * XL : (s + 1) * XL, y * LANES : (y + 1) * LANES] = lines[
                    s, pl.ds(y, XL, stride=YL), :
                ].astype(BF16)

    def reduce_and_send(t, g):
        for j in range(1, PX):
            rs_c[t, g, j].wait_recv()
        total = ybuf[t, g, ORDER.index(0)].astype(F32)
        for j in range(1, PX):
            total = total + rs[t, g, j - 1].astype(F32)
        for y in range(YL):
            turn[y * XROWS : (y + 1) * XROWS, :] = total[:, y * LANES : (y + 1) * LANES]
        for r in range(XROWS):
            sbuf[t, g, r * YL : (r + 1) * YL, :] = turn[pl.ds(r, YL, stride=XROWS), :].astype(BF16)
        mine = pl.ds(pl.multiple_of(py * PIECE, PIECE), PIECE)
        for k in range(1, PY):
            dest = lax.rem(py + k, PY)
            rows = pl.ds(pl.multiple_of(dest * PIECE, PIECE), PIECE)
            a2_c[2 * t, g, k] = send(
                sbuf.at[t, g, rows], rbuf.at[t, g, mine], a2_s.at[2 * t, g, k - 1], a2_r.at[2 * t, g, k - 1], at_py(k)
            )
        rbuf[t, g, mine, :] = sbuf[t, g, mine, :]

    def spectrum(t):
        for g in range(GROUPS):
            for k in range(1, PY):
                a2_c[2 * t, g, k].wait_recv()
        rows = jnp.concatenate([rbuf[t, g] for g in range(GROUPS)], axis=1)
        return dot(tab["my"][...], rows).astype(BF16)

    def spread(hat, which):
        part = slice(which * CH * MODES, (which + 1) * CH * MODES)
        chosen = dot(hat, tab["sel"][part, :]).astype(BF16)
        for b in range(HALF):
            us[b * ROWS : (b + 1) * ROWS, :] = chosen[:, b * 128 : (b + 1) * 128]
        for q in range(2):
            if which:
                ue[q, :, :PATTERN] = dot(us[...], tab["expand"][q, :, WIDE:]).astype(BF16)
            else:
                ue[q] = dot(us[...], tab["expand"][q, :, :WIDE]).astype(BF16)

    def mix(which, collapse):
        def body(n, _):
            q, b = n // HALF, lax.rem(n, HALF)
            re = pl.ds(pl.multiple_of(b * ROWS, ROWS), KY)
            im = pl.ds(pl.multiple_of(b * ROWS + KY, KY), KY)
            for v in range(WIDE // 128):
                cols = slice(v * 128, min((v + 1) * 128, IO))
                size = cols.stop - cols.start
                at = (v % 3) * 128 if which else v * 128
                w_re, w_im = w[q, re, cols].astype(F32), w[q, im, cols].astype(F32)
                u_re, u_im = ue[q, re, at : at + size].astype(F32), ue[q, im, at : at + size].astype(F32)
                if which:
                    prod[q, re, cols] = (w_re * u_re + w_im * u_im).astype(BF16)
                    prod[q, im, cols] = (w_re * u_im - w_im * u_re).astype(BF16)
                else:
                    prod[q, re, cols] = (w_re * u_re - w_im * u_im).astype(BF16)
                    prod[q, im, cols] = (w_re * u_im + w_im * u_re).astype(BF16)
            return 0

        lax.fori_loop(0, MODES, body, 0)
        summed = (dot(prod[0], collapse[0]) + dot(prod[1], collapse[1])).astype(BF16)
        lined = jnp.concatenate([summed[b * ROWS : (b + 1) * ROWS] for b in range(HALF)], axis=1)
        return dot(lined, tab["place"][...]).astype(BF16)

    own_block = pl.ds(pl.multiple_of(px * BLOCK, BLOCK), BLOCK)

    def inverse_send(t, mixed):
        spatial = dot(tab["myt"][...], mixed).astype(BF16)
        mine = pl.ds(pl.multiple_of(px * BLOCK + py * PIECE, PIECE), PIECE)
        for g in range(GROUPS):
            vbuf[t, g] = spatial[:, g * LANES : (g + 1) * LANES]
            for k in range(1, PY):
                dest = lax.rem(py + k, PY)
                rows = pl.ds(pl.multiple_of(dest * PIECE, PIECE), PIECE)
                a2_c[2 * t + 1, g, k] = send(
                    vbuf.at[t, g, rows], ag.at[t, g, mine],
                    a2_s.at[2 * t + 1, g, k - 1], a2_r.at[2 * t + 1, g, k - 1], at_py(k),
                )
            here = pl.ds(pl.multiple_of(py * PIECE, PIECE), PIECE)
            ag[t, g, mine, :] = vbuf[t, g, here, :]

    def gather_send(t, g):
        for k in range(1, PY):
            a2_c[2 * t + 1, g, k].wait_recv()
        for j in (2, 1, 3):
            ag_c[t, g, j] = send(
                ag.at[t, g, own_block], ag.at[t, g, own_block], ag_s.at[t, g, j - 1], ag_r.at[t, g, j - 1], at_px(j)
            )

    def cross_back(t, g):
        for j in range(1, PX):
            ag_c[t, g, j].wait_recv()

        group_values(
            ag[t, g], tab["m1t"], tab["dht" if t == 0 else "dzt"], wide_ag, xbuf, back, tbuf, zval
        )

    def bypass_part(matrix, source, target, first, last):
        def body(b, _):
            parts = []
            for e in range(2):
                rows = pl.ds(pl.multiple_of(b * 32 + e * 16, 16), 16)
                parts.append(source[:, rows, :].reshape(CH * YL, NZ))
            value = dot(matrix[...], jnp.concatenate(parts, axis=1))
            for e in range(2):
                rows = pl.ds(pl.multiple_of(b * 32 + e * 16, 16), 16)
                target[:, rows, :] = value[:, e * NZ : (e + 1) * NZ].reshape(CH, YL, NZ).astype(target.dtype)
            return 0

        lax.fori_loop(first, last, body, 0)

    def share(name, n, data):
        for j in range(1, 4):
            dp_c[name, j] = send(data.at[0], data.at[j], dp_s.at[n, j], dp_r.at[n, j], at_y(j))
        dp_c[name, 4] = send(data.at[0], data.at[4], dp_s.at[n, 4], dp_r.at[n, 4], far)

    def share_far(name, n, data):
        dp_c[name, 4].wait_recv()
        for j in range(1, 4):
            dp_c[name, 4 + j] = send(data.at[4], data.at[4 + j], dp_s.at[n, 4 + j], dp_r.at[n, 4 + j], at_y(j))

    need("f0", "dz", "m1")
    load("f1", fields_h.at[pl.ds(GC, GC)], fields.at[pl.ds(GC, GC)], 3)
    load("f2", fields_h.at[pl.ds(2 * GC, GC)], fields.at[pl.ds(2 * GC, GC)], 4)
    load("w", w_h, w4, 5)
    load("m1t", tab_h["m1t"].at[px], tab["m1t"], 6)
    for g in range(GROUPS):
        need("f%d" % g)
        if g == GROUPS - 1:
            load_later()

        depth(fields, g, tab["dz"])
        if g == 0:
            pl.semaphore_wait(barrier, len(partners))
        cross_and_send(0, g)

    need("rep", "rept")
    mask = lax.rem(lax.broadcasted_iota(jnp.int32, (CH * YL, CH * YL), 0), YL) == lax.rem(
        lax.broadcasted_iota(jnp.int32, (CH * YL, CH * YL), 1), YL
    )
    left = dot(tab["rep"][...], byp[...]).astype(BF16)
    full = dot(left, tab["rept"][...])
    bypk[...] = jnp.where(mask, full, 0.0).astype(BF16)
    bypkt[...] = jnp.where(mask, full, 0.0).T.astype(BF16)

    need("w")

    def weight_rows(b, _):
        for q in range(2):
            for part in range(2):
                w[q, pl.ds(pl.multiple_of(b * ROWS + part * KY, KY), KY), :] = w4[:, 2 * b + q, part, :]
        return 0

    lax.fori_loop(0, HALF // 2, weight_rows, 0)
    reduce_and_send(0, 0)
    lax.fori_loop(HALF // 2, HALF, weight_rows, 0)
    reduce_and_send(0, 1)
    reduce_and_send(0, 2)

    need("my", "sel", "expand", "sum_o", "place", "myt")
    u_hat = spectrum(0)
    dpu[0] = u_hat
    share("u", 0, dpu)
    spread(u_hat, 0)
    inverse_send(0, mix(0, tab["sum_o"]))
    bypass_part(bypk, fields, pb, 0, 9)
    need("m1t", "dht", "dh", "cot")
    for g in range(GROUPS):
        gather_send(0, g)
    share_far("u", 0, dpu)
    bypass_part(bypk, fields, pb, 9, CELLS // 32)

    for g in range(GROUPS):
        cross_back(0, g)

        def body(r, _):
            rows = pl.ds(pl.multiple_of(r * CHUNK, CHUNK), CHUNK)
            for c in range(GC):
                pre = zval[c, rows, :] + pb[g * GC + c, rows, :]
                slope = gelu_slope(pre)
                gp[g * GC + c, rows, :] = (cot[g * GC + c, rows, :].astype(F32) * slope).astype(BF16)
            return 0

        lax.fori_loop(0, CELLS // CHUNK, body, 0)
        depth(gp, g, tab["dh"])
        cross_and_send(1, g)
        if g:
            reduce_and_send(1, g - 1)
    bypass_part(bypkt, gp, pb16, 0, CELLS // 32)
    stores = [pltpu.make_async_copy(pb16.at[pl.ds(GC, 2 * GC)], pb_h, store_sem.at[0])]
    stores[0].start()
    reduce_and_send(1, GROUPS - 1)

    need("sum_i", "dzt")
    g_hat = spectrum(1)
    dpg[0] = g_hat
    share("g", 1, dpg)
    spread(g_hat, 1)
    inverse_send(1, mix(1, tab["sum_i"]))

    def choose(h):
        for j in range(NEAR * h, NEAR * (h + 1)):
            if j:
                if h == 0 or j > NEAR:
                    dp_c["u", j].wait_recv()
                    dp_c["g", j].wait_recv()
        part = slice(NEAR * h, NEAR * (h + 1))
        both = jnp.concatenate(
            [dpu[part].reshape(NEAR * ROWS, CH * MODES), dpg[part].reshape(NEAR * ROWS, CH * MODES)], axis=1
        )
        chosen = dot(both, tab["sel"][...]).astype(BF16)
        for b in range(HALF):
            gs[b] = chosen[:, b * 128 : (b + 1) * 128]

    def gw_part(h, first, last):
        def gw_body(b, _):
            for q in range(2):
                wide[...] = dot(gs[b], tab["expand"][q])
                for v in range(WIDE // 128):
                    cols = slice(v * 128, min((v + 1) * 128, IO))
                    size = cols.stop - cols.start
                    at = WIDE + (v % 3) * 128
                    real = acc[2 * b + q, 0, :, cols] if h else None
                    imag = acc[2 * b + q, 1, :, cols] if h else None
                    for d in range(NEAR):
                        re = slice(d * ROWS, d * ROWS + KY)
                        im = slice(d * ROWS + KY, (d + 1) * ROWS)
                        u_re, u_im = wide[re, cols], wide[im, cols]
                        g_re, g_im = wide[re, at : at + size], wide[im, at : at + size]
                        more_real = g_re * u_re + g_im * u_im
                        more_imag = g_im * u_re - g_re * u_im
                        real = more_real if real is None else real + more_real
                        imag = more_imag if imag is None else imag + more_imag
                    if h:
                        gw[:, 2 * b + q, 0, cols] = real
                        gw[:, 2 * b + q, 1, cols] = imag
                    else:
                        acc[2 * b + q, 0, :, cols] = real
                        acc[2 * b + q, 1, :, cols] = imag
            return 0

        lax.fori_loop(first, last, gw_body, 0)

    choose(0)
    gw_part(0, 0, 3)
    gather_send(1, 0)
    share_far("g", 1, dpg)
    gw_part(0, 3, 5)
    gather_send(1, 1)
    gather_send(1, 2)
    gw_part(0, 5, HALF)

    cross_back(1, 0)
    for h in range(2):
        add_bypass(zval, pb16, out, h * CELLS // CHUNK // 2, (h + 1) * CELLS // CHUNK // 2)
        part = (slice(None), pl.ds(h * CELLS // 2, CELLS // 2))
        stores.append(pltpu.make_async_copy(out.at[part], gf_h.at[part], store_sem.at[1 + h]))
        stores[-1].start()

    choose(1)
    gw_part(1, 0, HALF)
    stores.append(pltpu.make_async_copy(gw, gw_h, store_sem.at[3]))
    stores[-1].start()
    for g in range(1, GROUPS):
        for j in range(1, PX):
            ag_c[1, g, j].wait_recv()
        stores.append(pltpu.make_async_copy(ag.at[1, g], ag_h.at[g - 1], store_sem.at[3 + g]))
        stores[-1].start()

    for copy in stores:
        copy.wait()
    for copy in sends:
        copy.wait_send()


def last_groups(gw_in, gf_in, ag_in, pb_in, m1t_h, dzt_h, gw_out, gf_out,
                gw, gf, ag, pb, m1t, dzt, wide_ag, xbuf, back, tbuf, zval, sem, out_sem):
    px = lax.axis_index("px")
    pairs = [
        (ag_in.at[0], ag.at[0]), (m1t_h.at[px], m1t), (dzt_h, dzt),
        (pb_in.at[pl.ds(0, GC)], pb.at[pl.ds(0, GC)]), (gw_in, gw), (ag_in.at[1], ag.at[1]),
        (pb_in.at[pl.ds(GC, GC)], pb.at[pl.ds(GC, GC)]), (gf_in, gf.at[pl.ds(0, GC)]),
    ]
    reads = [pltpu.make_async_copy(src, dst, sem.at[n]) for n, (src, dst) in enumerate(pairs)]
    for read in reads[:4]:
        read.start()
    writes = []

    def write(src, dst):
        writes.append(pltpu.make_async_copy(src, dst, out_sem.at[len(writes)]))
        writes[-1].start()

    for n in range(3):
        reads[n].wait()
    for read in reads[4:]:
        read.start()
    for g in range(1, GROUPS):
        if g == 2:
            reads[5].wait()
        group_values(ag[g - 1], m1t, dzt, wide_ag, xbuf, back, tbuf, zval)
        reads[3 if g == 1 else 6].wait()
        part = pl.ds(g * GC, GC)
        if g == 1:
            reads[4].wait()
            write(gw, gw_out)
        for h in range(2):
            add_bypass(
                zval, pb.at[pl.ds((g - 1) * GC, GC)], gf.at[part],
                h * CELLS // CHUNK // 2, (h + 1) * CELLS // CHUNK // 2,
            )
            rows = pl.ds(h * CELLS // 2, CELLS // 2)
            write(gf.at[part, rows], gf_out.at[part, rows])
        if g == 1:
            reads[7].wait()
            write(gf.at[pl.ds(0, GC)], gf_out.at[pl.ds(0, GC)])
    for copy in writes:
        copy.wait()


def shards(fields, cotangent, spectral_weight, bypass):
    tab = tables()
    arrays = [jnp.asarray(tab[name]) for name in NAMES]
    any_spec = pl.BlockSpec(memory_space=pl.ANY)
    vmem = pltpu.VMEM
    shapes = [a.shape[1:] if name in ("m1", "m1t") else a.shape for name, a in zip(NAMES, arrays)]
    scratch = [vmem(shape, BF16) for shape in shapes] + [
        vmem((CH, CELLS, NZ), BF16),
        vmem((CH, CELLS, NZ), BF16),
        vmem((CH, CELLS, NZ), BF16),
        vmem((KY, MODES, 2, IO), BF16),
        vmem((2, HALF * ROWS, IO), BF16),
        vmem((CH, CELLS, NZ), F32),
        vmem((CH, CELLS, NZ), BF16),
        vmem((GC, CELLS, NZ), BF16),
        vmem((CH * YL, CH * YL), BF16),
        vmem((CH * YL, CH * YL), BF16),
        vmem((2 * XL, YLANES), BF16),
        vmem((CELLS, 2 * LANES), BF16),
        vmem((GC, CELLS, NZ), F32),
        vmem((2, CELLS, LANES), F32),
        vmem((YL * XROWS, LANES), F32),
        vmem((YL * 2 * XL, LANES), F32),
        vmem((2 * KX * YL, LANES), F32),
        vmem((2, GROUPS, PX, XROWS, YLANES), BF16),
        vmem((2, GROUPS, PX - 1, XROWS, YLANES), BF16),
        vmem((2, GROUPS, BLOCK, LANES), BF16),
        vmem((2, GROUPS, BLOCK, LANES), BF16),
        vmem((2, GROUPS, BLOCK, LANES), BF16),
        vmem((2, GROUPS, PX * BLOCK, LANES), BF16),
        vmem((DP, ROWS, CH * MODES), BF16),
        vmem((DP, ROWS, CH * MODES), BF16),
        vmem((2, HALF * ROWS, WIDE), BF16),
        vmem((2, HALF * ROWS, IO), BF16),
        vmem((HALF * ROWS, 128), BF16),
        vmem((HALF, NEAR * ROWS, 128), BF16),
        vmem((NEAR * ROWS, WIDE + PATTERN), F32),
        vmem((MODES, 2, KY, WIDE), F32),
        vmem((KY, MODES, 2, IO), F32),
        pltpu.SemaphoreType.DMA((len(NAMES) + 5,)),
        pltpu.SemaphoreType.DMA((6,)),
        pltpu.SemaphoreType.DMA((2, GROUPS, PX - 1)),
        pltpu.SemaphoreType.DMA((2, GROUPS, PX - 1)),
        pltpu.SemaphoreType.DMA((4, GROUPS, PY - 1)),
        pltpu.SemaphoreType.DMA((4, GROUPS, PY - 1)),
        pltpu.SemaphoreType.DMA((2, GROUPS, PX - 1)),
        pltpu.SemaphoreType.DMA((2, GROUPS, PX - 1)),
        pltpu.SemaphoreType.DMA((2, DP)),
        pltpu.SemaphoreType.DMA((2, DP)),
    ]
    gw, gf, ag, pb = pl.pallas_call(
        kernel,
        out_shape=(
            jax.ShapeDtypeStruct((KY, MODES, 2, IO), F32),
            jax.ShapeDtypeStruct((GC, CELLS, NZ), BF16),
            jax.ShapeDtypeStruct((2, PX * BLOCK, LANES), BF16),
            jax.ShapeDtypeStruct((2 * GC, CELLS, NZ), BF16),
        ),
        in_specs=[any_spec] * 3 + [pl.BlockSpec(memory_space=pltpu.VMEM)] + [any_spec] * len(arrays),
        out_specs=(any_spec,) * 4,
        scratch_shapes=scratch,
        compiler_params=pltpu.CompilerParams(
            collective_id=0, has_side_effects=True, vmem_limit_bytes=60 * 1024 * 1024
        ),
        cost_estimate=pl.CostEstimate(flops=20_000_000_000, bytes_accessed=30_000_000, transcendentals=3_000_000),
    )(
        fields.reshape(CH, CELLS, NZ), cotangent.reshape(CH, CELLS, NZ), spectral_weight, bypass, *arrays
    )
    gw, gf = pl.pallas_call(
        last_groups,
        out_shape=(
            jax.ShapeDtypeStruct((KY, MODES, 2, IO), F32),
            jax.ShapeDtypeStruct((CH, CELLS, NZ), BF16),
        ),
        in_specs=[any_spec] * 6,
        out_specs=(any_spec, any_spec),
        scratch_shapes=[
            vmem((KY, MODES, 2, IO), F32),
            vmem((CH, CELLS, NZ), BF16),
            vmem((2, PX * BLOCK, LANES), BF16),
            vmem((2 * GC, CELLS, NZ), BF16),
            vmem((2 * XL, 2 * KX), BF16),
            vmem((2 * LANES, GC * NZ), BF16),
            vmem((2 * KX * YL, LANES), F32),
            vmem((2 * XL, YLANES), BF16),
            vmem((YL * 2 * XL, LANES), F32),
            vmem((CELLS, 2 * LANES), BF16),
            vmem((GC, CELLS, NZ), F32),
            pltpu.SemaphoreType.DMA((8,)),
            pltpu.SemaphoreType.DMA((6,)),
        ],
        compiler_params=pltpu.CompilerParams(vmem_limit_bytes=56 * 1024 * 1024),
        cost_estimate=pl.CostEstimate(flops=1_000_000_000, bytes_accessed=12_000_000, transcendentals=0),
    )(gw, gf, ag, pb, jnp.asarray(tab["m1t"]), jnp.asarray(tab["dzt"]))
    return gw, gf.reshape(1, CH, XL, YL, NZ)


def solution(mesh):
    in_specs = (
        P("dp", None, "px", "py", None),
        P("dp", None, "px", "py", None),
        P(("px", "py"), None, None, None),
        P(),
    )
    out_specs = (P(("px", "py"), None, None, None), P("dp", None, "px", "py", None))
    return jax.shard_map(shards, mesh=mesh, in_specs=in_specs, out_specs=out_specs, check_vma=False)
```
